32 devices in a mesh: groups: 2 (over y), row: 16 (over z, x, core).
Axes of the slice: x: 2, y: 2, z: 4, core: 2. Of those that a mesh axis runs over, the one named last changes fastest.
Arguments:
- homolog_activation: float32 [32, 512, 256], P('groups', 'row'), parts along dimension 0, may hold values from -6 to 6
- homolog_entry_valid: int32 [32, 512], P('groups', 'row'), parts along dimension 0, may hold values 0 or 1
- amino_valid_flags: int32 [1024], P(('groups', 'row')), parts along dimension 0, may hold values 0 or 1
- first_factor_weights: float32 [256, 32], replicated, may hold values from -0.375 to 0.375
- second_factor_weights: float32 [256, 32], replicated, may hold values from -0.375 to 0.375
- final_linear_weights: float32 [1024, 128], replicated, may hold values from -0.1875 to 0.1875
- couple_delta_deriv: float32 [1024, 512, 128], P(('groups', 'row')), parts along dimension 0, may hold values from -6 to 6
Outputs:
- alignment_grad: float32 [32, 512, 256], P('groups', 'row'), parts along dimension 0
- left_weight_grad: float32 [512, 32], P('groups'), parts along dimension 0
- right_weight_grad: float32 [512, 32], P('groups'), parts along dimension 0
- out_weight_grad: float32 [2048, 128], P('groups'), parts along dimension 0
The draws below stay inside these ranges and needn't reach their ends.
There are 2 independent parts, one for each index of `groups`. The reference program is written for one: setup_inputs(seed, part) draws one part's arguments, and reference() takes and returns one part's arrays. A program takes and returns all parts, laid end to end along the dimension named above; an argument that names none is the same for every part. Nothing has to cross between parts.
All inputs are finite; a program needn't handle non-finite values. No bound on the sum of `homolog_entry_valid` or of `amino_valid_flags` on one device may be relied on, other than what follows from the above.
Results may differ from the reference program's by a relative error of at most 0.0003.
Values sent between devices are 32-bit elements; how exact they have to be, the bound alone decides.
No kernel may reach another device: no remote copies, remote signals or barrier semaphores. Data moves between devices by JAX's collectives and lax.ppermute only.
A program may use at most 128 MiB of HBM per device.

```python
import jax
import jax.numpy as jnp
from jax import lax

FAMILY_DIMS = 256
MAPPED_DIMS = 32
PAIR_CHANNELS = 128
AMINO_NUMBER = 512
HOMOLOG_NUMBER = 16


def with_ends(entries, stream_key, least, high):
    place = [jax.random.randint(jax.random.fold_in(stream_key, axis), (), 0, length) for axis, length in enumerate(entries.shape)]
    longest = entries.shape.index(max(entries.shape))
    beside = place[:longest] + [(place[longest] + 1) % entries.shape[longest]] + place[longest + 1:]
    return entries.at[tuple(place)].set(least).at[tuple(beside)].set(high)


def raised(array, stream_key, source, target, blocks, factor):
    owner, partner = [(jnp.arange(array.shape[dim]) // (array.shape[dim] // blocks)).reshape([-1 if axis == dim else 1 for axis in range(array.ndim)]) for dim in (source, target)]
    chosen = jax.random.permutation(stream_key, blocks)[partner]
    strong = (owner == chosen) | (owner == (partner + blocks // 2) % blocks)
    return jnp.where(strong, factor * array, array)


def block_levels(key, dims, cuts, least, largest):
    def one(position, blocks):
        heights = jax.random.uniform(jax.random.fold_in(jax.random.fold_in(key, 6), position), (blocks,), jnp.float32, least / len(cuts), largest / len(cuts))
        return jnp.repeat(jnp.exp(heights), dims[position] // blocks).reshape((-1,) + (1,) * (len(dims) - position - 1))

    loudness = one(*cuts[0])
    for cut in cuts[1:]:
        loudness = loudness * one(*cut)
    return loudness


def noise(key, extent, width, reach, cuts=(), kind=jnp.bfloat16):
    result = width * jax.random.normal(key, extent, jnp.float32)
    if cuts:
        result = result * block_levels(key, extent, cuts, -0.22, 0.18)
    return jnp.clip(result, -reach, reach).astype(kind)


def heavy_noise(own_key, dims, scale, reach, shards, heavy, held_as=jnp.bfloat16):
    result = scale * jax.random.normal(own_key, dims, jnp.float32)
    if shards:
        result = result * block_levels(own_key, dims, shards, -0.22, 0.18)
    return jnp.clip(raised(result, jax.random.fold_in(own_key, 3), *heavy), -reach, reach).astype(held_as)


def setup_inputs(seed: int = 0, part: int = 0) -> dict:
    splits = jax.random.split(jax.random.key(seed), 8)
    own_keys = jax.random.split(jax.random.fold_in(splits[7], part), 8)
    homolog_activation = noise(own_keys[0], (HOMOLOG_NUMBER, AMINO_NUMBER, FAMILY_DIMS), 1.0, 6.0, ((1, 16),), jnp.float32)
    homolog_entry_valid = with_ends((jax.random.randint(own_keys[1], (HOMOLOG_NUMBER, AMINO_NUMBER), 0, 2) < 1).astype(jnp.int32), jax.random.fold_in(own_keys[1], 1), 0, 1)
    amino_valid_flags = with_ends((jax.random.randint(own_keys[2], (AMINO_NUMBER,), 0, 8) < 7).astype(jnp.int32), jax.random.fold_in(own_keys[2], 1), 0, 1)
    first_factor_weights = noise(splits[3], (FAMILY_DIMS, MAPPED_DIMS), FAMILY_DIMS ** -0.5, 0.375, (), jnp.float32)
    second_factor_weights = noise(splits[4], (FAMILY_DIMS, MAPPED_DIMS), FAMILY_DIMS ** -0.5, 0.375, (), jnp.float32)
    final_linear_weights = noise(splits[5], (MAPPED_DIMS * MAPPED_DIMS, PAIR_CHANNELS), (MAPPED_DIMS * MAPPED_DIMS) ** -0.5, 0.1875, (), jnp.float32)
    couple_delta_deriv = heavy_noise(own_keys[6], (AMINO_NUMBER, AMINO_NUMBER, PAIR_CHANNELS), 1.0, 6.0, ((0, 16),), (0, 1, 16, 2.0), jnp.float32)
    return dict(homolog_activation=homolog_activation, homolog_entry_valid=homolog_entry_valid, amino_valid_flags=amino_valid_flags, first_factor_weights=first_factor_weights, second_factor_weights=second_factor_weights, final_linear_weights=final_linear_weights, couple_delta_deriv=couple_delta_deriv)


SPLIT_PIECES = lax.Precision.HIGHEST


def reference(homolog_activation, homolog_entry_valid, amino_valid_flags, first_factor_weights, second_factor_weights, final_linear_weights, couple_delta_deriv):
    keep_mask = homolog_entry_valid.astype(jnp.float32)
    validity_swapped = keep_mask.T
    present = amino_valid_flags.astype(jnp.float32)
    first_factor_embed = jnp.einsum('gsj,ju->sgu', homolog_activation, first_factor_weights, precision=SPLIT_PIECES) * validity_swapped[:, :, None]
    second_factor_embed = jnp.einsum('gsj,ju->sgu', homolog_activation, second_factor_weights, precision=SPLIT_PIECES) * validity_swapped[:, :, None]
    count = jnp.dot(validity_swapped, keep_mask, precision=SPLIT_PIECES, preferred_element_type=jnp.float32)
    factor = present[:, None] * present[None, :] / jnp.maximum(count, 1.0)
    w_three = final_linear_weights.reshape(MAPPED_DIMS, MAPPED_DIMS, PAIR_CHANNELS)
    stride = 64
    nblocks = AMINO_NUMBER // stride

    def step(carry, index):
        right_acc, out_acc = carry
        begin = (index * stride).astype(jnp.int32)
        grads = lax.dynamic_slice_in_dim(couple_delta_deriv, begin, stride, 0)
        grads = grads * lax.dynamic_slice_in_dim(factor, begin, stride, 0)[:, :, None]
        left_blk = lax.dynamic_slice_in_dim(first_factor_embed, begin, stride, 0)
        feats = jnp.einsum('ijk,abk->ijab', grads, w_three, precision=SPLIT_PIECES)
        left_part = jnp.einsum('ijab,jsb->isa', feats, second_factor_embed, precision=SPLIT_PIECES)
        right_acc = right_acc + jnp.einsum('ijab,isa->jsb', feats, left_blk, precision=SPLIT_PIECES)
        outer = jnp.einsum('isa,jsb->ijab', left_blk, second_factor_embed, precision=SPLIT_PIECES)
        out_acc = out_acc + jnp.einsum('ijab,ijk->abk', outer, grads, precision=SPLIT_PIECES)
        return (right_acc, out_acc), left_part

    start = (jnp.zeros((AMINO_NUMBER, HOMOLOG_NUMBER, MAPPED_DIMS), jnp.float32), jnp.zeros((MAPPED_DIMS, MAPPED_DIMS, PAIR_CHANNELS), jnp.float32))
    (second_factor_embed_deriv, output_grad), parts = lax.scan(step, start, jnp.arange(nblocks, dtype=jnp.int32))
    first_factor_embed_deriv = parts.reshape(AMINO_NUMBER, HOMOLOG_NUMBER, MAPPED_DIMS) * validity_swapped[:, :, None]
    second_factor_embed_deriv = second_factor_embed_deriv * validity_swapped[:, :, None]
    alignment_grad = jnp.einsum('ztp,fp->tzf', first_factor_embed_deriv, first_factor_weights, precision=SPLIT_PIECES) + jnp.einsum('ztp,fp->tzf', second_factor_embed_deriv, second_factor_weights, precision=SPLIT_PIECES)
    first_operand_array = jnp.einsum('zea,ezi->ai', homolog_activation, first_factor_embed_deriv, precision=SPLIT_PIECES)
    second_operand_array = jnp.einsum('zea,ezi->ai', homolog_activation, second_factor_embed_deriv, precision=SPLIT_PIECES)
    return (alignment_grad, first_operand_array, second_operand_array, output_grad.reshape(MAPPED_DIMS * MAPPED_DIMS, PAIR_CHANNELS))
```

```python
import functools

import jax
import jax.numpy as jnp
from jax import lax
from jax.experimental import pallas as pl
from jax.experimental.pallas import tpu as pltpu
from jax.sharding import PartitionSpec as P

EXACT = lax.Precision.HIGHEST

F32, BF16 = jnp.float32, jnp.bfloat16
NT = (((1,), (1,)), ((), ()))
NN = (((1,), (0,)), ((), ()))
TN = (((0,), (0,)), ((), ()))

def split(x):
    hi = x.astype(BF16)
    return hi, (x - hi.astype(F32)).astype(BF16)

def split_outside(x):
    hi = lax.reduce_precision(x, 8, 7)
    return hi.astype(BF16), (x - hi).astype(BF16)


def dot(a, b, dims=NN):
    return lax.dot_general(a, b, dims, preferred_element_type=F32)

def params(mib, sem=None):
    return pltpu.CompilerParams(vmem_limit_bytes=mib << 20)

def t_kernel(lcat_ref, wcat_ref, thi_ref, tlo_ref, *, ib, s, w, k):
    t = dot(lcat_ref[...], wcat_ref[...])
    hi, lo = split(t)
    for i in range(ib):
        for b in range(w):
            thi_ref[b*s:(b+1)*s, i*k:(i+1)*k] = hi[i*s:(i+1)*s, b*k:(b+1)*k]
            tlo_ref[b*s:(b+1)*s, i*k:(i+1)*k] = lo[i*s:(i+1)*s, b*k:(b+1)*k]

def t_call(lcat, wcat, r, s, w, k, ib):
    return pl.pallas_call(
        functools.partial(t_kernel, ib=ib, s=s, w=w, k=k),
        grid=(r // ib,),
        in_specs=[pl.BlockSpec((ib*s, lcat.shape[1]), lambda g: (g, 0)),
                  pl.BlockSpec(wcat.shape, lambda g: (0, 0))],
        out_specs=[pl.BlockSpec((w*s, ib*k), lambda g: (0, g))]*2,
        out_shape=[jax.ShapeDtypeStruct((w*s, r*k), BF16)]*2,
        compiler_params=params(48), name="t_call")(lcat, wcat)

def g_block(me, d_ref, f_ref, offs, r, i, o):
    src = pl.multiple_of((me ^ offs[o]) * r, r)
    return d_ref[i, pl.ds(src, r), :] * f_ref[0, o*r:(o+1)*r, i:i+1]

def b_kernel(me_ref, d_ref, f_ref, thi_ref, tlo_ref, out_ref, ghi, glo, *, ib, offs, r, k, part, parts, chunk):
    me = me_ref[0]
    n = len(offs)
    per = n // parts
    @pl.when(pl.program_id(0) == 0)
    def _():
        out_ref[...] = jnp.zeros_like(out_ref)
    cb = chunk // r
    for c in range(per // cb):
        for q in range(cb):
            o = c*cb + q
            for i in range(ib):
                hi, lo = split(g_block(me, d_ref, f_ref, offs, r, i, part*per + o))
                ghi[o*r:(o+1)*r, i*k:(i+1)*k] = hi
                glo[o*r:(o+1)*r, i*k:(i+1)*k] = lo
        sl = slice(c*chunk, (c+1)*chunk)
        out_ref[sl] += (dot(ghi[sl], thi_ref[...], NT) + dot(ghi[sl], tlo_ref[...], NT) + dot(glo[sl], thi_ref[...], NT))

def b_call(me, d, ft, thi, tlo, offs, rb, ib, part, parts, chunk):
    r, total, k = d.shape
    ws = thi.shape[0]
    rows = total // parts
    return pl.pallas_call(
        functools.partial(b_kernel, ib=ib, offs=offs, r=rb, k=k, part=part, parts=parts, chunk=chunk),
        grid=(r // ib,),
        in_specs=[pl.BlockSpec(memory_space=pltpu.SMEM),
                  pl.BlockSpec((ib, total, k), lambda g: (g, 0, 0)),
                  pl.BlockSpec((1, total, ib), lambda g: (g, 0, 0)),
                  pl.BlockSpec((ws, ib*k), lambda g: (0, g)),
                  pl.BlockSpec((ws, ib*k), lambda g: (0, g))],
        out_specs=pl.BlockSpec((rows, ws), lambda g: (0, 0)),
        out_shape=jax.ShapeDtypeStruct((rows, ws), F32),
        scratch_shapes=[pltpu.VMEM((rows, ib*k), BF16)]*2,
        compiler_params=params(48), name=f"b_call{part}")(me, d, ft, thi, tlo)

def c_kernel(me_ref, d_ref, f_ref, rg_ref, whi_ref, wlo_ref, lt_ref, lg_ref, ow_ref, rhi, rlo, ghi, glo, xhi, xlo, *, ib, offs, r, s, w, k, chunk):
    me = me_ref[0]
    n = len(offs)
    @pl.when(pl.program_id(0) == 0)
    def _():
        ow_ref[...] = jnp.zeros_like(ow_ref)
        hi, lo = split(rg_ref[...].T)
        rhi[...] = hi
        rlo[...] = lo
    ci = chunk // k
    for c in range(ib // ci):
        for i in range(c*ci, (c+1)*ci):
            for o in range(n):
                hi, lo = split(g_block(me, d_ref, f_ref, offs, r, i, o))
                ghi[o*r:(o+1)*r, i*k:(i+1)*k] = hi
                glo[o*r:(o+1)*r, i*k:(i+1)*k] = lo
        sl = slice(c*chunk, (c+1)*chunk)
        c1 = dot(rhi[...], ghi[:, sl]) + dot(rhi[...], glo[:, sl]) + dot(rlo[...], ghi[:, sl])
        hi, lo = split(c1)
        for i in range(c*ci, (c+1)*ci):
            ii = i - c*ci
            for b in range(w):
                xhi[i*s:(i+1)*s, b*k:(b+1)*k] = hi[b*s:(b+1)*s, ii*k:(ii+1)*k]
                xlo[i*s:(i+1)*s, b*k:(b+1)*k] = lo[b*s:(b+1)*s, ii*k:(ii+1)*k]
    lg_ref[...] = dot(xhi[...], whi_ref[...], NT) + dot(xhi[...], wlo_ref[...], NT) + dot(xlo[...], whi_ref[...], NT)
    lhi, llo = split(lt_ref[0])
    ow_ref[...] += dot(lhi, xhi[...]) + dot(llo, xhi[...]) + dot(lhi, xlo[...])

def c_call(me, d, ft, rg, whi, wlo, lt, offs, rb, ib, s, chunk):
    r, total, k = d.shape
    w = whi.shape[0]
    ws = w*s
    return pl.pallas_call(
        functools.partial(c_kernel, ib=ib, offs=offs, r=rb, s=s, w=w, k=k, chunk=chunk),
        grid=(r // ib,),
        in_specs=[pl.BlockSpec(memory_space=pltpu.SMEM),
                  pl.BlockSpec((ib, total, k), lambda g: (g, 0, 0)),
                  pl.BlockSpec((1, total, ib), lambda g: (g, 0, 0)),
                  pl.BlockSpec((total, ws), lambda g: (0, 0)),
                  pl.BlockSpec((w, w*k), lambda g: (0, 0)),
                  pl.BlockSpec((w, w*k), lambda g: (0, 0)),
                  pl.BlockSpec((1, w, ib*s), lambda g: (g, 0, 0))],
        out_specs=[pl.BlockSpec((ib*s, w), lambda g: (g, 0)), pl.BlockSpec((w, w*k), lambda g: (0, 0))],
        out_shape=[jax.ShapeDtypeStruct((r*s, w), F32), jax.ShapeDtypeStruct((w, w*k), F32)],
        scratch_shapes=[pltpu.VMEM((ws, total), BF16)]*2 + [pltpu.VMEM((total, ib*k), BF16)]*2 + [pltpu.VMEM((ib*s, w*k), BF16)]*2,
        compiler_params=params(56), name="c_call")(me, d, ft, rg, whi, wlo, lt)


def swap(x, bit, n):
    return lax.ppermute(x, "row", [(i, i ^ bit) for i in range(n)])


def gather_relative(x, bits, n):
    for bit in bits:
        x = jnp.concatenate([x, swap(x, bit, n)], axis=0)
    return x


def relative_order(bits):
    offs = [0]
    for bit in bits:
        offs = offs + [o ^ bit for o in offs]
    return tuple(offs)


def local(n, activation, valid, flags, w1, w2, wf, delta):
    s, r, m = activation.shape
    total, k = delta.shape[1:]
    w = w1.shape[1]
    ib = min(8, r)
    groups = r // ib
    me = lax.axis_index("row").astype(jnp.int32)
    bits = [1 << e for e in reversed(range(n.bit_length() - 1))]
    offs = relative_order(bits)

    keep = valid.astype(F32)
    present = flags.astype(F32)
    masks = gather_relative(jnp.concatenate([keep.reshape(-1), present])[None], bits, n)
    keep_rel = masks[:, : s * r].reshape(n, s, r)
    present_rel = masks[:, s * r :].reshape(total)
    count = lax.dot_general(
        keep_rel.astype(BF16), keep.astype(BF16), (((1,), (0,)), ((), ())), preferred_element_type=F32
    ).reshape(total, r)
    ft = present_rel[:, None] * present[None, :] / jnp.maximum(count, 1.0)
    ft = ft.reshape(total, groups, ib).transpose(1, 0, 2)

    both = jnp.einsum("sim,mc->isc", activation, jnp.concatenate([w1, w2], axis=1), precision=EXACT)
    both = both * keep.T[:, :, None]
    left, right = both[:, :, :w], both[:, :, w:]
    right_own = right.transpose(0, 2, 1).reshape(1, r, w * s)
    right_rel = gather_relative(right_own, bits, n).reshape(total, w * s)

    wcat = wf.reshape(w, w * k)
    whi, wlo = split_outside(wcat)
    lflat = left.reshape(r * s, w)
    lhi, llo = split_outside(lflat)
    thi, tlo = t_call(
        jnp.concatenate([lhi, llo, lhi], axis=1), jnp.concatenate([whi, whi, wlo], axis=0), r, s, w, k, ib
    )

    if r % 16 == 0:
        where, rb, blocks = me.reshape(1), r, offs
    else:
        order = me ^ jnp.array(offs, jnp.int32)
        delta = jnp.take(delta.reshape(r, n, r, k), order, axis=1).reshape(r, total, k)
        rb = 128
        where, blocks = jnp.zeros((1,), jnp.int32), tuple(range(total // rb))

    far = b_call(where, delta, ft, thi, tlo, blocks, rb, ib, 1, 2, 256)
    near = b_call(where, delta, ft, thi, tlo, blocks, rb, ib, 0, 2, 256)

    quarter = w // 4
    places = (0, 2, 1, 3)
    turn = (me & 3) ^ jnp.array(places, jnp.int32)
    lt = jnp.take(lflat.T.reshape(4, quarter, r * s), turn, axis=0).reshape(w, groups, ib * s).transpose(1, 0, 2)
    left_grad, ow = c_call(where, delta, ft, right_rel, whi, wlo, lt, blocks, rb, ib, s, 256)

    grad = near + swap(far, 1, n)
    for bit in reversed(bits[:-1]):
        half = grad.shape[0] // 2
        grad = grad[:half] + swap(grad[half:], bit, n)
    half = w // 2
    ow = ow[:half] + swap(ow[half:], 1, n)
    ow = ow[:quarter] + swap(ow[quarter:], 2, n)
    for bit in reversed(bits[:-2]):
        ow = ow + swap(ow, bit, n)
    ow = jnp.concatenate([ow, swap(ow, 2, n)], axis=0)
    ow = jnp.concatenate([ow, swap(ow, 1, n)], axis=0)
    back = jnp.array(places, jnp.int32)[(me & 3) ^ jnp.arange(4, dtype=jnp.int32)]
    out_grad = jnp.take(ow.reshape(4, quarter, w * k), back, axis=0).reshape(w * w, k)

    right_grad = grad.reshape(r, w, s).transpose(2, 0, 1) * keep[:, :, None]
    left_grad = left_grad.reshape(r, s, w).transpose(1, 0, 2) * keep[:, :, None]
    grads = jnp.concatenate([left_grad, right_grad], axis=2)
    alignment = jnp.einsum("sic,mc->sim", grads, jnp.concatenate([w1, w2], axis=1), precision=EXACT)
    small = jnp.einsum("sim,sic->cm", activation, grads, precision=EXACT)
    for bit in reversed(bits):
        small = small + swap(small, bit, n)
    return alignment, small[:w].T, small[w:].T, out_grad


def solution(mesh):
    in_specs = (
        P("groups", "row", None),
        P("groups", "row"),
        P(("groups", "row")),
        P(),
        P(),
        P(),
        P(("groups", "row"), None, None),
    )
    out_specs = (P("groups", "row", None), P("groups", None), P("groups", None), P("groups", None))
    body = functools.partial(local, mesh.shape["row"])
    return jax.shard_map(body, mesh=mesh, in_specs=in_specs, out_specs=out_specs, check_vma=False)
```

```python
import functools

import jax
import jax.numpy as jnp
from jax import lax
from jax.experimental import pallas as pl
from jax.experimental.pallas import tpu as pltpu
from jax.sharding import PartitionSpec as P

EXACT = lax.Precision.HIGHEST
F32, BF16 = jnp.float32, jnp.bfloat16
NT = (((1,), (1,)), ((), ()))
NN = (((1,), (0,)), ((), ()))
VM = pl.BlockSpec(memory_space=pltpu.VMEM)
SM = pl.BlockSpec(memory_space=pltpu.SMEM)
ANY = pl.BlockSpec(memory_space=pl.ANY)


def split(x):
    hi = x.astype(BF16)
    return hi, (x - hi.astype(F32)).astype(BF16)


def split_outside(x):
    hi = lax.reduce_precision(x, 8, 7)
    return hi.astype(BF16), (x - hi).astype(BF16)


def dot(a, b, dims=NN):
    return lax.dot_general(a, b, dims, preferred_element_type=F32)


def call(kernel, name, cost_us, mib, **kw):
    return pl.pallas_call(
        kernel,
        compiler_params=pltpu.CompilerParams(vmem_limit_bytes=mib << 20),
        cost_estimate=pl.CostEstimate(flops=int(cost_us * 1e9), bytes_accessed=0, transcendentals=0),
        name=name,
        **kw,
    )


def t_kernel(lcat_ref, wcat_ref, d_ref, thi_ref, tlo_ref, dv_ref, sem, *, ib, s, w, k, r):
    copy = pltpu.make_async_copy(d_ref, dv_ref, sem)
    copy.start()
    for g in range(r // ib):
        hi, lo = split(dot(lcat_ref[g * ib * s : (g + 1) * ib * s, :], wcat_ref[...]))
        for i in range(ib):
            q = g * ib + i
            for b in range(w):
                rows, lanes = slice(i * s, (i + 1) * s), slice(b * k, (b + 1) * k)
                thi_ref[b * s : (b + 1) * s, q * k : (q + 1) * k] = hi[rows, lanes]
                tlo_ref[b * s : (b + 1) * s, q * k : (q + 1) * k] = lo[rows, lanes]
    copy.wait()


def t_call(lcat, wcat, d, s, w, ib):
    r, total, k = d.shape
    return call(
        functools.partial(t_kernel, ib=ib, s=s, w=w, k=k, r=r),
        "left_by_weights",
        3.4,
        40,
        in_specs=[VM, VM, ANY],
        out_specs=[VM] * 3,
        out_shape=[pltpu.VMEM((w * s, r * k), BF16)] * 2 + [pltpu.VMEM(d.shape, F32)],
        scratch_shapes=[pltpu.SemaphoreType.DMA],
    )(lcat, wcat, d)


def b_kernel(me_ref, d_ref, f_ref, thi_ref, tlo_ref, out_ref, ghi, glo, *, ib, offs, rb, k, part, parts, steps):
    me = me_ref[0]
    per = len(offs) // parts
    rows = per * rb

    def prep(g):
        for o in range(per):
            at = part * per + o
            src = pl.multiple_of((me ^ offs[at]) * rb, rb)
            for i in range(ib):
                q = g * ib + i
                x = d_ref[q, pl.ds(src, rb), :] * f_ref[g, at * rb : (at + 1) * rb, i : i + 1]
                hi, lo = split(x)
                ghi[o * rb : (o + 1) * rb, q * k : (q + 1) * k] = hi
                glo[o * rb : (o + 1) * rb, q * k : (q + 1) * k] = lo

    prep(0)
    for g in range(steps):
        if g + 1 < steps:
            prep(g + 1)
        lanes = slice(g * ib * k, (g + 1) * ib * k)
        hi, lo = ghi[:, lanes], glo[:, lanes]
        x = dot(jnp.concatenate([hi, lo], axis=0), thi_ref[:, lanes], NT)
        x = x[:rows] + x[rows:] + dot(hi, tlo_ref[:, lanes], NT)
        out_ref[...] = x if g == 0 else out_ref[...] + x


def b_call(me, d, ft, thi, tlo, offs, rb, ib, part, parts):
    r, total, k = d.shape
    ws = thi.shape[0]
    rows = total // parts
    return call(
        functools.partial(b_kernel, ib=ib, offs=offs, rb=rb, k=k, part=part, parts=parts, steps=r // ib),
        f"right_grad_{part}",
        3.5,
        8,
        in_specs=[SM, VM, VM, VM, VM],
        out_specs=[VM] * 3,
        out_shape=[pltpu.VMEM((rows, ws), F32)] + [pltpu.VMEM((rows, r * k), BF16)] * 2,
    )(me, d, ft, thi, tlo)


def c_kernel(*refs, ib, s, k, steps, blocks, part, parts):
    g_refs = refs[: 2 * blocks]
    rg_ref, w_ref, lt_ref, lg_ref, ow_ref, rr, xhi, xlo, acc = refs[2 * blocks :]
    ws = rg_ref.shape[1] // parts
    wk = w_ref.shape[1] // parts
    w = lt_ref.shape[0] // 2
    rows = g_refs[0].shape[0]
    hi, lo = split(rg_ref[:, part * ws : (part + 1) * ws].T)
    rr[:ws] = hi
    rr[ws:] = lo

    def first(g):
        lanes = slice(g * ib * k, (g + 1) * ib * k)
        c1 = 0.0
        for p in range(blocks):
            js = slice(p * rows, (p + 1) * rows)
            x = dot(rr[:, js], g_refs[2 * p][:, lanes])
            c1 = c1 + x[:ws] + x[ws:] + dot(rr[:ws, js], g_refs[2 * p + 1][:, lanes])
        hi, lo = split(c1)
        for i in range(ib):
            q = g * ib + i
            for b in range(ws // s):
                xhi[q * s : (q + 1) * s, b * k : (b + 1) * k] = hi[b * s : (b + 1) * s, i * k : (i + 1) * k]
                xlo[q * s : (q + 1) * s, b * k : (b + 1) * k] = lo[b * s : (b + 1) * s, i * k : (i + 1) * k]

    def second(q0, q1):
        at = slice(q0 * ib * s, q1 * ib * s)
        xh, xl = xhi[at], xlo[at]
        mine = slice(part * wk, (part + 1) * wk)
        x = dot(xh, w_ref[:, mine], NT)
        lg_ref[at] = x[:, :w] + x[:, w:] + dot(xl, w_ref[:w, mine], NT)
        x = dot(lt_ref[:, at], xh)
        x = x[:w] + x[w:] + dot(lt_ref[:w, at], xl)
        x = x if q0 == 0 else acc[...] + x
        if q1 < steps:
            acc[...] = x
        else:
            for b in range(ws // s):
                ow_ref[:, b, :] = x[:, b * k : (b + 1) * k]

    span = min(2, steps)
    for g in range(steps):
        first(g)
        if g >= span and g % span == 0:
            second(g - span, g)
    second(steps - span, steps)


def c_call(gs, rg, w2, lt2, ib, s, k, part, parts):
    blocks = len(gs) // 2
    total, ws = rg.shape
    ws = ws // parts
    w = lt2.shape[0] // 2
    r = gs[0].shape[1] // k
    wk = w2.shape[1] // parts
    return call(
        functools.partial(c_kernel, ib=ib, s=s, k=k, steps=r // ib, blocks=blocks, part=part, parts=parts),
        f"left_and_weight_grad_{part}",
        5.6,
        20,
        in_specs=[VM] * (2 * blocks + 3),
        out_specs=[VM] * 2,
        out_shape=[pltpu.VMEM((r * s, w), F32), pltpu.VMEM((w, ws // s, k), F32)],
        scratch_shapes=[pltpu.VMEM((2 * ws, total), BF16)]
        + [pltpu.VMEM((r * s, wk), BF16)] * 2
        + [pltpu.VMEM((w, wk), F32)],
    )(*gs, rg, w2, lt2)


def swap(x, bit, n):
    return lax.ppermute(x, "row", [(i, i ^ bit) for i in range(n)])


def gather_relative(x, bits, n):
    for bit in bits:
        x = jnp.concatenate([x, swap(x, bit, n)], axis=0)
    return x


def relative_order(bits):
    offs = [0]
    for bit in bits:
        offs = offs + [o ^ bit for o in offs]
    return tuple(offs)


def pick(x, index):
    return x.at[index].get(mode="promise_in_bounds")


def after(x, *others):
    return lax.optimization_barrier((x, *others))[0]


def local(n, activation, valid, flags, w1, w2, wf, delta):
    s, r, m = activation.shape
    total, k = delta.shape[1:]
    w = w1.shape[1]
    ib = min(8, r)
    groups = r // ib
    parts = 2
    me = lax.axis_index("row").astype(jnp.int32)
    bits = [1 << e for e in reversed(range(n.bit_length() - 1))]
    offs = relative_order(bits)

    keep = valid.astype(F32)
    present = flags.astype(F32)
    both = jnp.einsum("sim,mc->isc", activation, jnp.concatenate([w1, w2], axis=1), precision=EXACT)
    both = both * keep.T[:, :, None]
    left, right = both[:, :, :w], both[:, :, w:]
    right_own = right.transpose(0, 2, 1).reshape(1, r, w * s)

    masks = jnp.concatenate([valid.reshape(-1), flags])[None]
    right_rel = right_own
    for step, bit in enumerate(bits):
        masks = jnp.concatenate([masks, swap(masks, bit, n)], axis=0)
        if step < len(bits) - 2:
            right_rel = jnp.concatenate([right_rel, swap(right_rel, bit, n)], axis=0)
    keep_rel = masks[:, : s * r].reshape(n, s, r)
    present_rel = masks[:, s * r :].reshape(total).astype(F32)
    count = lax.dot_general(
        keep_rel.astype(BF16), keep.astype(BF16), (((1,), (0,)), ((), ())), preferred_element_type=F32
    ).reshape(total, r)
    ft = present_rel[:, None] * present[None, :] / jnp.maximum(count, 1.0)
    ft = ft.reshape(total, groups, ib).transpose(1, 0, 2)
    early = right_rel
    right_rel = jnp.concatenate([right_rel, swap(right_rel, 2, n)], axis=0)

    whi, wlo = split_outside(wf.reshape(w, w * k))
    lflat = left.reshape(r * s, w)
    lhi, llo = split_outside(lflat)

    if r % 16 == 0:
        where, rb, blocks = me.reshape(1), r, offs
    else:
        order = me ^ jnp.array(offs, jnp.int32)
        delta = jnp.take(delta.reshape(r, n, r, k), order, axis=1).reshape(r, total, k)
        rb = total // 4
        where, blocks = jnp.zeros((1,), jnp.int32), tuple(range(4))

    thi, tlo, delta = t_call(
        after(jnp.concatenate([lhi, llo, lhi], axis=1), ft, early), jnp.concatenate([whi, whi, wlo], axis=0), delta, s, w, ib
    )
    right_rel_half = right_rel
    right_rel = jnp.concatenate([right_rel, swap(right_rel, 1, n)], axis=0).reshape(total, w * s)
    far, fhi, flo = b_call(where, delta, ft, thi, tlo, blocks, rb, ib, 1, 2)
    near, nhi, nlo = b_call(where, delta, ft, thi, tlo, blocks, rb, ib, 0, 2)

    quarter = w // 4
    places = (0, 2, 1, 3)
    turn = (me & 3) ^ jnp.array(places, jnp.int32)
    lt = pick(lflat.T.reshape(4, quarter, r * s), turn).reshape(w, r * s)
    lt2 = jnp.concatenate(split_outside(lt), axis=0)
    wboth = jnp.concatenate([whi, wlo], axis=0)

    left_grad = 0.0
    ows = []
    for part in range(parts):
        lg, ow = c_call((nhi, nlo, fhi, flo), right_rel, wboth, lt2, ib, s, k, part, parts)
        left_grad = left_grad + lg
        half = w // 2
        ow = ow[:half] + swap(ow[half:], 1, n)
        lt2 = after(lt2, ow)
        ow = ow[:quarter] + swap(ow[quarter:], 2, n)
        for bit in reversed(bits[:-2]):
            ow = ow + swap(ow, bit, n)
        ow = jnp.concatenate([ow, swap(ow, 2, n)], axis=0)
        ow = jnp.concatenate([ow, swap(ow, 1, n)], axis=0)
        ows.append(ow)

    grad = after(near + swap(far, 1, n), right_rel_half)
    for bit in reversed(bits[:-1]):
        half = grad.shape[0] // 2
        grad = grad[:half] + swap(grad[half:], bit, n)

    right_grad = grad.reshape(r, w, s).transpose(2, 0, 1) * keep[:, :, None]
    left_grad = left_grad.reshape(r, s, w).transpose(1, 0, 2) * keep[:, :, None]
    grads = jnp.concatenate([left_grad, right_grad], axis=2)
    alignment = jnp.einsum("sic,mc->sim", grads, jnp.concatenate([w1, w2], axis=1), precision=EXACT)
    small = jnp.einsum("sim,sic->cm", activation, grads, precision=EXACT)
    for bit in reversed(bits):
        small = small + swap(small, bit, n)

    back = pick(jnp.array(places, jnp.int32), (me & 3) ^ jnp.arange(4, dtype=jnp.int32))
    out_grad = jnp.concatenate(ows, axis=1).reshape(4, quarter, w, k)
    out_grad = pick(out_grad, back).reshape(w * w, k)
    return alignment, small[:w].T, small[w:].T, out_grad


def solution(mesh):
    in_specs = (
        P("groups", "row", None),
        P("groups", "row"),
        P(("groups", "row")),
        P(),
        P(),
        P(),
        P(("groups", "row"), None, None),
    )
    out_specs = (P("groups", "row", None), P("groups", None), P("groups", None), P("groups", None))
    body = functools.partial(local, mesh.shape["row"])
    return jax.shard_map(body, mesh=mesh, in_specs=in_specs, out_specs=out_specs, check_vma=False)
```

```python
import functools

import jax
import jax.numpy as jnp
from jax import lax
from jax.experimental import pallas as pl
from jax.experimental.pallas import tpu as pltpu
from jax.sharding import PartitionSpec as P

EXACT = lax.Precision.HIGHEST
F32, BF16 = jnp.float32, jnp.bfloat16
NT = (((1,), (1,)), ((), ()))
NN = (((1,), (0,)), ((), ()))
PLACES = (0, 2, 1, 3)
GAP = 32
VM = pl.BlockSpec(memory_space=pltpu.VMEM)
SM = pl.BlockSpec(memory_space=pltpu.SMEM)
ANY = pl.BlockSpec(memory_space=pl.ANY)


def split(x):
    hi = x.astype(BF16)
    return hi, (x - hi.astype(F32)).astype(BF16)


def split_outside(x):
    hi = lax.reduce_precision(x, 8, 7)
    return hi.astype(BF16), (x - hi).astype(BF16)


def dot(a, b, dims=NN):
    return lax.dot_general(a, b, dims, preferred_element_type=F32)


def weights(w_ref, w, first=0, size=None):
    return jnp.concatenate([w_ref[pl.ds(b, w, stride=w), :] for b in range(first, first + (size or w))], axis=1)


def residues(l_ref, r, s, first, size):
    return jnp.concatenate([l_ref[pl.ds(i, s, stride=r), :] for i in range(first, first + size)], axis=0)


def call(kernel, name, cost_us, mib, **kw):
    return pl.pallas_call(
        kernel,
        compiler_params=pltpu.CompilerParams(vmem_limit_bytes=mib << 20),
        cost_estimate=pl.CostEstimate(flops=int(cost_us * 1e9), bytes_accessed=0, transcendentals=0),
        name=name,
        **kw,
    )


def b_kernel(
    me_ref, d_ref, m_ref, own_ref, l_ref, w_ref, oa_ref, ob_ref, ahi, alo, bhi, blo, thi_ref, tlo_ref, dv_ref, f_ref, wcat, sem, *, ib, offs, rb, s
):
    r, total, k = d_ref.shape
    w = l_ref.shape[1]
    steps = r // ib
    per = len(offs) // 2
    copy = pltpu.make_async_copy(d_ref, dv_ref, sem)
    copy.start()
    me = me_ref[0]

    every = m_ref[...].astype(BF16)
    lane = lax.broadcasted_iota(jnp.int32, own_ref.shape, 1)
    for p in range(2):
        own = own_ref[...] if p == 0 else pltpu.roll(own_ref[...], GAP, 1)
        keep = jnp.where((lane >= p * GAP) & (lane < p * GAP + s), own, 0.0).astype(BF16)
        present = jnp.where(lane == p * GAP + s, own, 0.0).astype(BF16)
        f_ref[p] = dot(every, present, NT) / jnp.maximum(dot(every, keep, NT), 1.0)

    hi, lo = split(weights(w_ref, w))
    wcat[:w] = hi
    wcat[w : 2 * w] = hi
    wcat[2 * w :] = lo
    for g in range(steps):
        left = residues(l_ref, r, s, g * ib, ib)
        hi = left.astype(BF16).astype(F32)
        hi, lo = split(dot(jnp.concatenate([hi, left - hi, hi], axis=1).astype(BF16), wcat[...]))
        for i in range(ib):
            q = g * ib + i
            for b in range(w):
                rows, lanes = slice(i * s, (i + 1) * s), slice(b * k, (b + 1) * k)
                thi_ref[b * s : (b + 1) * s, q * k : (q + 1) * k] = hi[rows, lanes]
                tlo_ref[b * s : (b + 1) * s, q * k : (q + 1) * k] = lo[rows, lanes]
    copy.wait()

    def scale(p, ghi, glo, g):
        for o in range(per):
            src = pl.multiple_of((me ^ offs[p * per + o]) * rb, rb)
            for q in range(g * ib, (g + 1) * ib):
                hi, lo = split(dv_ref[q, pl.ds(src, rb), :] * f_ref[p, o * rb : (o + 1) * rb, q : q + 1])
                ghi[o * rb : (o + 1) * rb, q * k : (q + 1) * k] = hi
                glo[o * rb : (o + 1) * rb, q * k : (q + 1) * k] = lo

    work = [(p, halves, g) for p, halves in ((1, (ob_ref, bhi, blo)), (0, (oa_ref, ahi, alo))) for g in range(steps)]

    def prepare(p, halves, g):
        scale(p, halves[1], halves[2], g)

    prepare(*work[0])
    for t, (p, (out_ref, ghi, glo), g) in enumerate(work):
        if t + 1 < len(work):
            prepare(*work[t + 1])
        lanes = slice(g * ib * k, (g + 1) * ib * k)
        hi, lo = ghi[:, lanes], glo[:, lanes]
        rows = hi.shape[0]
        x = dot(jnp.concatenate([hi, lo], axis=0), thi_ref[:, lanes], NT)
        x = x[:rows] + x[rows:] + dot(hi, tlo_ref[:, lanes], NT)
        out_ref[...] = x if g == 0 else out_ref[...] + x


def b_call(me, d, masks, own, left, w, offs, rb, ib, s):
    r, total, k = d.shape
    ws = left.shape[1] * s
    rows = total // 2
    return call(
        functools.partial(b_kernel, ib=ib, offs=offs, rb=rb, s=s),
        "right_grad",
        11.0,
        30,
        in_specs=[SM, ANY, VM, VM, VM, VM],
        out_specs=[VM] * 6,
        out_shape=[pltpu.VMEM((rows, ws), F32)] * 2 + [pltpu.VMEM((rows, r * k), BF16)] * 4,
        scratch_shapes=[pltpu.VMEM((ws, r * k), BF16)] * 2
        + [
            pltpu.VMEM(d.shape, F32),
            pltpu.VMEM((2, rows, r), F32),
            pltpu.VMEM((3 * left.shape[1], left.shape[1] * k), BF16),
            pltpu.SemaphoreType.DMA,
        ],
    )(me, pltpu.with_memory_space_constraint(d, pltpu.HBM), masks, own, left, w)


def c_kernel(*refs, ib, s, k, steps, blocks, part, parts):
    g_refs = refs[: 2 * blocks]
    me_ref, ra_ref, rb_ref, w_ref, l_ref, lg_ref, keep_ref, send_ref, rr, xhi, xlo, acc, lt_ref, turned, wsplit = refs[2 * blocks :]
    w = l_ref.shape[1]
    wk = w * k // parts
    ws = w * s // parts
    rows = g_refs[0].shape[0]
    hi, lo = split(weights(w_ref, w, part * w // parts, w // parts))
    wsplit[:w] = hi
    wsplit[w:] = lo
    turned[...] = residues(l_ref, l_ref.shape[0] // s, s, 0, l_ref.shape[0] // s).T
    quarter = w // 4
    for t, place in enumerate(PLACES):
        at = pl.multiple_of(((me_ref[0] & 3) ^ place) * quarter, quarter)
        hi, lo = split(turned[pl.ds(at, quarter), :])
        lt_ref[t * quarter : (t + 1) * quarter] = hi.astype(F32)
        lt_ref[w + t * quarter : w + (t + 1) * quarter] = lo.astype(F32)
    for p, half in enumerate((ra_ref, rb_ref)):
        hi, lo = split(half[:, part * ws : (part + 1) * ws].T)
        rr[:ws, p * rows : (p + 1) * rows] = hi
        rr[ws:, p * rows : (p + 1) * rows] = lo

    def first(g):
        lanes = slice(g * ib * k, (g + 1) * ib * k)
        c1 = 0.0
        for p in range(blocks):
            js = slice(p * rows, (p + 1) * rows)
            x = dot(rr[:, js], g_refs[2 * p][:, lanes])
            c1 = c1 + x[:ws] + x[ws:] + dot(rr[:ws, js], g_refs[2 * p + 1][:, lanes])
        hi, lo = split(c1)
        for i in range(ib):
            q = g * ib + i
            for b in range(ws // s):
                xhi[q * s : (q + 1) * s, b * k : (b + 1) * k] = hi[b * s : (b + 1) * s, i * k : (i + 1) * k]
                xlo[q * s : (q + 1) * s, b * k : (b + 1) * k] = lo[b * s : (b + 1) * s, i * k : (i + 1) * k]

    def second(q0, q1):
        at = slice(q0 * ib * s, q1 * ib * s)
        xh, xl = xhi[at], xlo[at]
        x = dot(xh, wsplit[...], NT)
        lg_ref[at] = x[:, :w] + x[:, w:] + dot(xl, wsplit[:w], NT)
        lt = lt_ref[:, at].astype(BF16)
        x = dot(lt, xh)
        x = x[:w] + x[w:] + dot(lt[:w], xl)
        x = x if q0 == 0 else acc[...] + x
        if q1 < steps:
            acc[...] = x
        else:
            for b in range(ws // s):
                lanes = slice(b * k, (b + 1) * k)
                keep_ref[:, b, :] = x[: w // 2, lanes]
                send_ref[:, b, :] = x[w // 2 :, lanes]

    span = min(2, steps)
    for g in range(steps):
        first(g)
        if g >= span and g % span == 0:
            second(g - span, g)
    second(steps - span, steps)


def c_call(gs, me, rights, w2, left, ib, s, part, parts):
    blocks = len(gs) // 2
    total = 2 * rights[0].shape[0]
    w = left.shape[1]
    ws = w * s // parts
    k = w2.shape[1]
    r = gs[0].shape[1] // k
    wk = w * k // parts
    return call(
        functools.partial(c_kernel, ib=ib, s=s, k=k, steps=r // ib, blocks=blocks, part=part, parts=parts),
        f"left_and_weight_grad_{part}",
        5.6,
        20,
        in_specs=[VM] * (2 * blocks) + [SM, VM, VM, VM, VM],
        out_specs=[VM] * 3,
        out_shape=[pltpu.VMEM((r * s, w), F32)] + [pltpu.VMEM((w // 2, ws // s, k), F32)] * 2,
        scratch_shapes=[pltpu.VMEM((2 * ws, total), BF16)]
        + [pltpu.VMEM((r * s, wk), BF16)] * 2
        + [pltpu.VMEM((w, wk), F32), pltpu.VMEM((2 * w, r * s), F32), pltpu.VMEM((w, r * s), F32)]
        + [pltpu.VMEM((2 * w, wk), BF16)],
    )(*gs, me, *rights, w2, left)


def swap(x, bit, n):
    return lax.ppermute(x, "row", [(i, i ^ bit) for i in range(n)])


def gather_relative(x, bits, n):
    for bit in bits:
        x = jnp.concatenate([x, swap(x, bit, n)], axis=0)
    return x


def relative_order(bits):
    offs = [0]
    for bit in bits:
        offs = offs + [o ^ bit for o in offs]
    return tuple(offs)


def pick(x, index):
    return x.at[index].get(mode="promise_in_bounds")


def after(x, *others):
    return lax.optimization_barrier((x, *others))[0]


def local(n, activation, valid, flags, w1, w2, wf, delta):
    s, r, m = activation.shape
    total, k = delta.shape[1:]
    w = w1.shape[1]
    ib = min(8, r)
    parts = 2
    me = lax.axis_index("row").astype(jnp.int32)
    bits = [1 << e for e in reversed(range(n.bit_length() - 1))]
    offs = relative_order(bits)

    here = me.reshape(1)
    keep = valid.astype(F32)
    both = jnp.einsum("sim,mc->sic", activation, jnp.concatenate([w1, w2], axis=1), precision=EXACT)
    both = both * keep[:, :, None]
    left, right = both[:, :, :w].reshape(s * r, w), both[:, :, w:]
    ws = w * s
    own = jnp.concatenate([keep.T, flags.astype(F32)[:, None], jnp.zeros((r, GAP - 1 - s), F32)], axis=1)
    own = jnp.concatenate([own, swap(own, 1, n), jnp.zeros((r, k - 2 * GAP), F32)], axis=1)
    load = jnp.concatenate([right.transpose(1, 2, 0).reshape(r, ws), own], axis=1)
    for bit in bits[:-2]:
        other = swap(load, bit, n)
        masks = jnp.concatenate([load[:, ws:], other[:, ws:]], axis=0)
        load = jnp.concatenate([load, other], axis=0)
    masks = jnp.concatenate([masks, swap(masks, 2, n)], axis=0)
    load = after(load[:, :ws], masks)

    if r % 16 == 0:
        where, rb, blocks = here, r, offs
    else:
        order = me ^ jnp.array(offs, jnp.int32)
        delta = jnp.take(delta.reshape(r, n, r, k), order, axis=1).reshape(r, total, k)
        rb = total // 4
        where, blocks = jnp.zeros((1,), jnp.int32), tuple(range(4))

    near, far, *gs = b_call(where, delta, masks, own, left, wf, blocks, rb, ib, s)
    load = jnp.concatenate([load, after(swap(load, 2, n), near)], axis=0)
    rights = (load, swap(load, 1, n))

    def halves(x, y, rows):
        return x[:rows] + y[:rows], x[rows:] + y[rows:]

    later = list(reversed(bits[:-1]))
    rows = near.shape[0] // 2
    grad, send = halves(near, swap(far, 1, n), rows)
    left_a, ow_a, send_a = c_call(gs, after(here, grad, send), rights, wf, left, ib, s, 0, parts)
    other_a = swap(send_a, 1, n)
    rows = rows // 2
    grad, send = halves(grad, after(swap(send, later[0], n), left_a), rows)
    left_b, ow_b, send_b = c_call(gs, after(here, grad, send), rights, wf, left, ib, s, 1, parts)

    quarter = w // 4
    ow_b = ow_b + swap(send_b, 1, n)
    ow_a = ow_a + after(other_a, left_b)
    ow = jnp.concatenate([ow_a[:quarter], ow_b[:quarter]], axis=1)
    ow_send = jnp.concatenate([ow_a[quarter:], ow_b[quarter:]], axis=1)
    for bit in later[1:]:
        rows = rows // 2
        other = after(swap(send, bit, n), left_b)
        if bit == later[-1]:
            grad = grad + other
        else:
            grad, send = halves(grad, other, rows)
            send = after(send, ow_send)

    left_grad = (left_a + left_b).reshape(r, s, w).transpose(1, 0, 2) * keep[:, :, None]
    right_grad = grad.reshape(r, w, s).transpose(2, 0, 1) * keep[:, :, None]
    grads = jnp.concatenate([left_grad, right_grad], axis=2)
    alignment = jnp.einsum("sic,mc->sim", grads, jnp.concatenate([w1, w2], axis=1), precision=EXACT)
    small = jnp.einsum("sim,sic->cm", activation, grads, precision=EXACT)
    small = jnp.concatenate([small[:, i : i + k] for i in range(0, m, k)], axis=0).reshape(-1, w, k)
    ow = ow + swap(ow_send, 2, n)
    size = small.shape[0]
    ow = jnp.concatenate([small, ow], axis=0)
    for bit in reversed(bits[:-2]):
        ow = ow + swap(ow, bit, n)
    for bit in (2, 1):
        other = swap(ow, bit, n)
        ow = jnp.concatenate([ow[:size] + other[:size], ow[size:], other[size:]], axis=0)
    small = ow[:size].reshape(m // k, 2 * w, k).transpose(1, 0, 2).reshape(2 * w, m)

    back = pick(jnp.array(PLACES, jnp.int32), (me & 3) ^ jnp.arange(4, dtype=jnp.int32))
    out_grad = ow[size:].reshape(4, quarter, w, k)
    out_grad = pick(out_grad, back).reshape(w * w, k)
    return alignment, small[:w].T, small[w:].T, out_grad


def solution(mesh):
    in_specs = (
        P("groups", "row", None),
        P("groups", "row"),
        P(("groups", "row")),
        P(),
        P(),
        P(),
        P(("groups", "row"), None, None),
    )
    out_specs = (P("groups", "row", None), P("groups", None), P("groups", None), P("groups", None))
    body = functools.partial(local, mesh.shape["row"])
    return jax.shard_map(body, mesh=mesh, in_specs=in_specs, out_specs=out_specs, check_vma=False)
```

```python
import functools

import jax
import jax.numpy as jnp
from jax import lax
from jax.experimental import pallas as pl
from jax.experimental.pallas import tpu as pltpu
from jax.sharding import PartitionSpec as P

EXACT = lax.Precision.HIGHEST
F32, BF16 = jnp.float32, jnp.bfloat16
NT = (((1,), (1,)), ((), ()))
NN = (((1,), (0,)), ((), ()))
PLACES = (0, 2, 1, 3)
GAP = 32
VM = pl.BlockSpec(memory_space=pltpu.VMEM)
SM = pl.BlockSpec(memory_space=pltpu.SMEM)
ANY = pl.BlockSpec(memory_space=pl.ANY)


def split(x):
    hi = x.astype(BF16)
    return hi, (x - hi.astype(F32)).astype(BF16)


def split_outside(x):
    hi = lax.reduce_precision(x, 8, 7)
    return hi.astype(BF16), (x - hi).astype(BF16)


def dot(a, b, dims=NN):
    return lax.dot_general(a, b, dims, preferred_element_type=F32)


def weights(w_ref, w, first=0, size=None):
    return jnp.concatenate([w_ref[pl.ds(b, w, stride=w), :] for b in range(first, first + (size or w))], axis=1)


def residues(l_ref, r, s, first, size):
    return jnp.concatenate([l_ref[pl.ds(i, s, stride=r), :] for i in range(first, first + size)], axis=0)


def call(kernel, name, cost_us, mib, **kw):
    return pl.pallas_call(
        kernel,
        compiler_params=pltpu.CompilerParams(vmem_limit_bytes=mib << 20),
        cost_estimate=pl.CostEstimate(flops=int(cost_us * 1e9), bytes_accessed=0, transcendentals=0),
        name=name,
        **kw,
    )


def t_kernel(l_ref, w_ref, d_ref, thi_ref, tlo_ref, dv_ref, wcat, sem, *, ib, s):
    r, total, k = d_ref.shape
    w = l_ref.shape[1]
    copy = pltpu.make_async_copy(d_ref, dv_ref, sem)
    copy.start()
    hi, lo = split(weights(w_ref, w))
    wcat[:w] = hi
    wcat[w : 2 * w] = hi
    wcat[2 * w :] = lo
    for g in range(r // ib):
        left = residues(l_ref, r, s, g * ib, ib)
        hi = left.astype(BF16).astype(F32)
        hi, lo = split(dot(jnp.concatenate([hi, left - hi, hi], axis=1).astype(BF16), wcat[...]))
        for i in range(ib):
            q = g * ib + i
            for b in range(w):
                rows, lanes = slice(i * s, (i + 1) * s), slice(b * k, (b + 1) * k)
                thi_ref[b * s : (b + 1) * s, q * k : (q + 1) * k] = hi[rows, lanes]
                tlo_ref[b * s : (b + 1) * s, q * k : (q + 1) * k] = lo[rows, lanes]
    copy.wait()


def t_call(d, left, wf, ib, s):
    r, total, k = d.shape
    w = left.shape[1]
    return call(
        functools.partial(t_kernel, ib=ib, s=s),
        "left_by_weights",
        4.0,
        12,
        in_specs=[VM, VM, ANY],
        out_specs=[VM] * 3,
        out_shape=[pltpu.VMEM((w * s, r * k), BF16)] * 2 + [pltpu.VMEM(d.shape, F32)],
        scratch_shapes=[pltpu.VMEM((3 * w, w * k), BF16), pltpu.SemaphoreType.DMA],
    )(left, wf, pltpu.with_memory_space_constraint(d, pltpu.HBM))


def b_kernel(me_ref, dv, thi_ref, tlo_ref, m_ref, own_ref, out_ref, ghi, glo, f_ref, *, ib, offs, rb, s, part):
    r, total, k = dv.shape
    per = len(offs) // 2
    steps = r // ib
    me = me_ref[0]

    every = m_ref[...].astype(BF16)
    lane = lax.broadcasted_iota(jnp.int32, own_ref.shape, 1)
    p = part
    size = every.shape[0]
    for h in range(2):
        start = (2 * h + p) * GAP
        own = pltpu.roll(own_ref[...], start, 1) if start else own_ref[...]
        keep = jnp.where((lane >= start) & (lane < start + s), own, 0.0).astype(BF16)
        present = jnp.where(lane == start + s, own, 0.0).astype(BF16)
        f_ref[h * size : (h + 1) * size] = dot(every, present, NT) / jnp.maximum(dot(every, keep, NT), 1.0)

    def prepare(g):
        for o in range(per):
            src = pl.multiple_of((me ^ offs[p * per + o]) * rb, rb)
            for q in range(g * ib, (g + 1) * ib):
                hi, lo = split(dv[q, pl.ds(src, rb), :] * f_ref[o * rb : (o + 1) * rb, q : q + 1])
                ghi[o * rb : (o + 1) * rb, q * k : (q + 1) * k] = hi
                glo[o * rb : (o + 1) * rb, q * k : (q + 1) * k] = lo

    prepare(0)
    for g in range(steps):
        if g + 1 < steps:
            prepare(g + 1)
        lanes = slice(g * ib * k, (g + 1) * ib * k)
        hi, lo = ghi[:, lanes], glo[:, lanes]
        rows = hi.shape[0]
        x = dot(jnp.concatenate([hi, lo], axis=0), thi_ref[:, lanes], NT)
        x = x[:rows] + x[rows:] + dot(hi, tlo_ref[:, lanes], NT)
        out_ref[...] = x if g == 0 else out_ref[...] + x


def b_call(me, d, thi, tlo, masks, own, offs, rb, ib, s, part):
    r, total, k = d.shape
    ws = thi.shape[0]
    rows = total // 2
    held = [pltpu.with_memory_space_constraint(x, pltpu.VMEM) for x in (d, thi, tlo)]
    return call(
        functools.partial(b_kernel, ib=ib, offs=offs, rb=rb, s=s, part=part),
        f"right_grad_{part}",
        3.7,
        6,
        in_specs=[SM] + [VM] * 5,
        out_specs=[VM] * 3,
        out_shape=[pltpu.VMEM((rows, ws), F32)] + [pltpu.VMEM((rows, r * k), BF16)] * 2,
        scratch_shapes=[pltpu.VMEM((rows, r), F32)],
    )(me, *held, masks, own)


def c_kernel(*refs, ib, s, k, steps, blocks, part, parts):
    g_refs = refs[: 2 * blocks]
    me_ref, ra_ref, rb_ref, w_ref, l_ref, lg_ref, keep_ref, send_ref, rr, xhi, xlo, acc, lt_ref, turned, wsplit = refs[2 * blocks :]
    w = l_ref.shape[1]
    wk = w * k // parts
    ws = w * s // parts
    rows = g_refs[0].shape[0]
    hi, lo = split(weights(w_ref, w, part * w // parts, w // parts))
    wsplit[:w] = hi
    wsplit[w:] = lo
    turned[...] = residues(l_ref, l_ref.shape[0] // s, s, 0, l_ref.shape[0] // s).T
    quarter = w // 4
    for t, place in enumerate(PLACES):
        at = pl.multiple_of(((me_ref[0] & 3) ^ place) * quarter, quarter)
        hi, lo = split(turned[pl.ds(at, quarter), :])
        lt_ref[t * quarter : (t + 1) * quarter] = hi.astype(F32)
        lt_ref[w + t * quarter : w + (t + 1) * quarter] = lo.astype(F32)
    for p, half in enumerate((ra_ref, rb_ref)):
        hi, lo = split(half[:, part * ws : (part + 1) * ws].T)
        rr[:ws, p * rows : (p + 1) * rows] = hi
        rr[ws:, p * rows : (p + 1) * rows] = lo

    def first(g):
        lanes = slice(g * ib * k, (g + 1) * ib * k)
        c1 = 0.0
        for p in range(blocks):
            js = slice(p * rows, (p + 1) * rows)
            x = dot(rr[:, js], g_refs[2 * p][:, lanes])
            c1 = c1 + x[:ws] + x[ws:] + dot(rr[:ws, js], g_refs[2 * p + 1][:, lanes])
        hi, lo = split(c1)
        for i in range(ib):
            q = g * ib + i
            for b in range(ws // s):
                xhi[q * s : (q + 1) * s, b * k : (b + 1) * k] = hi[b * s : (b + 1) * s, i * k : (i + 1) * k]
                xlo[q * s : (q + 1) * s, b * k : (b + 1) * k] = lo[b * s : (b + 1) * s, i * k : (i + 1) * k]

    def second(q0, q1):
        at = slice(q0 * ib * s, q1 * ib * s)
        xh, xl = xhi[at], xlo[at]
        x = dot(xh, wsplit[...], NT)
        lg_ref[at] = x[:, :w] + x[:, w:] + dot(xl, wsplit[:w], NT)
        lt = lt_ref[:, at].astype(BF16)
        x = dot(lt, xh)
        x = x[:w] + x[w:] + dot(lt[:w], xl)
        x = x if q0 == 0 else acc[...] + x
        if q1 < steps:
            acc[...] = x
        else:
            for b in range(ws // s):
                lanes = slice(b * k, (b + 1) * k)
                keep_ref[:, b, :] = x[: w // 2, lanes]
                send_ref[:, b, :] = x[w // 2 :, lanes]

    span = min(2, steps)
    for g in range(steps):
        first(g)
        if g >= span and g % span == 0:
            second(g - span, g)
    second(steps - span, steps)


def c_call(gs, me, rights, w2, left, ib, s, part, parts):
    blocks = len(gs) // 2
    total = 2 * rights[0].shape[0]
    w = left.shape[1]
    ws = w * s // parts
    k = w2.shape[1]
    r = gs[0].shape[1] // k
    wk = w * k // parts
    return call(
        functools.partial(c_kernel, ib=ib, s=s, k=k, steps=r // ib, blocks=blocks, part=part, parts=parts),
        f"left_and_weight_grad_{part}",
        5.6,
        20,
        in_specs=[VM] * (2 * blocks) + [SM, VM, VM, VM, VM],
        out_specs=[VM] * 3,
        out_shape=[pltpu.VMEM((r * s, w), F32)] + [pltpu.VMEM((w // 2, ws // s, k), F32)] * 2,
        scratch_shapes=[pltpu.VMEM((2 * ws, total), BF16)]
        + [pltpu.VMEM((r * s, wk), BF16)] * 2
        + [pltpu.VMEM((w, wk), F32), pltpu.VMEM((2 * w, r * s), F32), pltpu.VMEM((w, r * s), F32)]
        + [pltpu.VMEM((2 * w, wk), BF16)],
    )(*gs, me, *rights, w2, left)


def swap(x, bit, n):
    return lax.ppermute(x, "row", [(i, i ^ bit) for i in range(n)])


def gather_relative(x, bits, n):
    for bit in bits:
        x = jnp.concatenate([x, swap(x, bit, n)], axis=0)
    return x


def relative_order(bits):
    offs = [0]
    for bit in bits:
        offs = offs + [o ^ bit for o in offs]
    return tuple(offs)


def pick(x, index):
    return x.at[index].get(mode="promise_in_bounds")


def after(x, *others):
    return lax.optimization_barrier((x, *others))[0]


def local(n, activation, valid, flags, w1, w2, wf, delta):
    s, r, m = activation.shape
    total, k = delta.shape[1:]
    w = w1.shape[1]
    ib = min(8, r)
    parts = 2
    me = lax.axis_index("row").astype(jnp.int32)
    bits = [1 << e for e in reversed(range(n.bit_length() - 1))]
    offs = relative_order(bits)

    here = me.reshape(1)
    keep = valid.astype(F32)
    both = jnp.einsum("sim,mc->sic", activation, jnp.concatenate([w1, w2], axis=1), precision=EXACT)
    both = both * keep[:, :, None]
    left, right = both[:, :, :w].reshape(s * r, w), both[:, :, w:]
    ws = w * s
    own = jnp.concatenate([valid, flags[None], jnp.zeros((GAP - 1 - s, r), jnp.int32)], axis=0)
    for bit in (1, 2):
        own = jnp.concatenate([own, swap(own, bit, n)], axis=0)
    own = own.T.astype(F32)
    masks = own
    load = jnp.concatenate([right.transpose(1, 2, 0).reshape(r, ws), own], axis=1)
    for bit in bits[:-2]:
        other = swap(load, bit, n)
        masks = jnp.concatenate([masks, other[:, ws:]], axis=0)
        load = jnp.concatenate([load[:, :ws], other[:, :ws]] if bit == bits[-3] else [load, other], axis=0)

    if r % 16 == 0:
        where, rb, blocks = here, r, offs
    else:
        order = me ^ jnp.array(offs, jnp.int32)
        delta = jnp.take(delta.reshape(r, n, r, k), order, axis=1).reshape(r, total, k)
        rb = total // 4
        where, blocks = jnp.zeros((1,), jnp.int32), tuple(range(4))

    thi, tlo, delta = t_call(delta, after(left, masks), wf, ib, s)
    far, fhi, flo = b_call(where, delta, thi, tlo, masks, own, blocks, rb, ib, s, 1)
    load = jnp.concatenate([load, after(swap(load, 2, n), far)], axis=0)
    near, nhi, nlo = b_call(after(where, load), delta, thi, tlo, masks, own, blocks, rb, ib, s, 0)
    gs = (nhi, nlo, fhi, flo)
    rights = (load, after(swap(load, 1, n), near))

    def halves(x, y, rows):
        return x[:rows] + y[:rows], x[rows:] + y[rows:]

    later = list(reversed(bits[:-1]))
    quarter = w // 4
    rows = near.shape[0] // 2
    grad, send = halves(near, after(swap(far, 1, n), near), rows)
    left_a, ow_a, send_a = c_call(gs, after(here, grad, send), rights, wf, left, ib, s, 0, parts)
    other_a = swap(send_a, 1, n)
    rows = rows // 2
    grad, send = halves(grad, after(swap(send, later[0], n), left_a), rows)
    ow_a, send_a = halves(ow_a, other_a, quarter)
    left_b, ow_b, send_b = c_call(gs, after(here, grad, send, ow_a, send_a), rights, wf, left, ib, s, 1, parts)

    ow_a = ow_a + after(swap(send_a, 2, n), left_b)
    ow_b, send_b = halves(ow_b, swap(send_b, 1, n), quarter)
    for bit in later[1:]:
        rows = rows // 2
        other = after(swap(send, bit, n), left_b)
        if bit == later[-1]:
            grad = grad + other
        else:
            grad, send = halves(grad, other, rows)
    ow_b = ow_b + swap(send_b, 2, n)

    left_grad = (left_a + left_b).reshape(r, s, w).transpose(1, 0, 2) * keep[:, :, None]
    right_grad = grad.reshape(r, w, s).transpose(2, 0, 1) * keep[:, :, None]
    grads = jnp.concatenate([left_grad, right_grad], axis=2)
    alignment = jnp.einsum("sic,mc->sim", grads, jnp.concatenate([w1, w2], axis=1), precision=EXACT)
    small = jnp.einsum("sim,sic->cm", activation, grads, precision=EXACT)

    def finish(x):
        for bit in reversed(bits[:-2]):
            x = x + swap(x, bit, n)
        for bit in (2, 1):
            x = jnp.concatenate([x, swap(x, bit, n)], axis=0)
        return x

    ow = jnp.concatenate([finish(ow_a), finish(ow_b)], axis=1)
    for bit in reversed(bits):
        small = small + swap(small, bit, n)

    back = (me & 3) ^ jnp.arange(4, dtype=jnp.int32)
    back = ((back & 1) << 1) | (back >> 1)
    out_grad = ow.reshape(4, quarter, w, k)
    out_grad = pick(out_grad, back).reshape(w * w, k)
    return alignment, small[:w].T, small[w:].T, out_grad


def solution(mesh):
    in_specs = (
        P("groups", "row", None),
        P("groups", "row"),
        P(("groups", "row")),
        P(),
        P(),
        P(),
        P(("groups", "row"), None, None),
    )
    out_specs = (P("groups", "row", None), P("groups", None), P("groups", None), P("groups", None))
    body = functools.partial(local, mesh.shape["row"])
    return jax.shard_map(body, mesh=mesh, in_specs=in_specs, out_specs=out_specs, check_vma=False)
```

```python
import functools

import jax
import jax.numpy as jnp
from jax import lax
from jax.experimental import pallas as pl
from jax.experimental.pallas import tpu as pltpu
from jax.experimental.layout import Layout, with_layout_constraint
from jax.sharding import PartitionSpec as P

EXACT = lax.Precision.HIGHEST
F32, BF16 = jnp.float32, jnp.bfloat16
NT = (((1,), (1,)), ((), ()))
NN = (((1,), (0,)), ((), ()))
PLACES = (0, 2, 1, 3)
GAP = 32
VM = pl.BlockSpec(memory_space=pltpu.VMEM)
SM = pl.BlockSpec(memory_space=pltpu.SMEM)
ANY = pl.BlockSpec(memory_space=pl.ANY)


def split(x):
    hi = x.astype(BF16)
    return hi, (x - hi.astype(F32)).astype(BF16)


def split_outside(x):
    hi = lax.reduce_precision(x, 8, 7)
    return hi.astype(BF16), (x - hi).astype(BF16)


def dot(a, b, dims=NN):
    return lax.dot_general(a, b, dims, preferred_element_type=F32)


def weights(w_ref, w, first=0, size=None):
    return jnp.concatenate([w_ref[pl.ds(b, w, stride=w), :] for b in range(first, first + (size or w))], axis=1)


def residues(l_ref, r, s, first, size):
    return jnp.concatenate([l_ref[pl.ds(i, s, stride=r), :] for i in range(first, first + size)], axis=0)


def call(kernel, name, cost_us, mib, **kw):
    return pl.pallas_call(
        kernel,
        compiler_params=pltpu.CompilerParams(vmem_limit_bytes=mib << 20),
        cost_estimate=pl.CostEstimate(flops=int(cost_us * 1e9), bytes_accessed=0, transcendentals=0),
        name=name,
        **kw,
    )


def t_kernel(l_ref, w_ref, d_ref, thi_ref, tlo_ref, dv_ref, wcat, sem, *, ib, s):
    r, total, k = d_ref.shape
    w = l_ref.shape[1]
    copy = pltpu.make_async_copy(d_ref, dv_ref, sem)
    copy.start()
    hi, lo = split(weights(w_ref, w))
    wcat[:w] = hi
    wcat[w : 2 * w] = hi
    wcat[2 * w :] = lo
    for g in range(r // ib):
        left = residues(l_ref, r, s, g * ib, ib)
        hi = left.astype(BF16).astype(F32)
        hi, lo = split(dot(jnp.concatenate([hi, left - hi, hi], axis=1).astype(BF16), wcat[...]))
        for i in range(ib):
            q = g * ib + i
            for b in range(w):
                rows, lanes = slice(i * s, (i + 1) * s), slice(b * k, (b + 1) * k)
                thi_ref[b * s : (b + 1) * s, q * k : (q + 1) * k] = hi[rows, lanes]
                tlo_ref[b * s : (b + 1) * s, q * k : (q + 1) * k] = lo[rows, lanes]
    copy.wait()


def t_call(d, left, wf, ib, s):
    r, total, k = d.shape
    w = left.shape[1]
    return call(
        functools.partial(t_kernel, ib=ib, s=s),
        "left_by_weights",
        4.0,
        12,
        in_specs=[VM, VM, ANY],
        out_specs=[VM] * 3,
        out_shape=[pltpu.VMEM((w * s, r * k), BF16)] * 2 + [pltpu.VMEM(d.shape, F32)],
        scratch_shapes=[pltpu.VMEM((3 * w, w * k), BF16), pltpu.SemaphoreType.DMA],
    )(left, wf, pltpu.with_memory_space_constraint(d, pltpu.HBM))


def b_kernel(me_ref, dv, thi_ref, tlo_ref, m_ref, own_ref, out_ref, ghi, glo, f_ref, *, ib, offs, rb, s, part):
    r, total, k = dv.shape
    per = len(offs) // 2
    steps = r // ib
    me = me_ref[0]

    every = m_ref[...].astype(BF16)
    lane = lax.broadcasted_iota(jnp.int32, own_ref.shape, 1)
    p = part
    size = every.shape[0]
    for h in range(2):
        start = (2 * h + p) * GAP
        own = pltpu.roll(own_ref[...], start, 1) if start else own_ref[...]
        keep = jnp.where((lane >= start) & (lane < start + s), own, 0.0).astype(BF16)
        present = jnp.where(lane == start + s, own, 0.0).astype(BF16)
        f_ref[h * size : (h + 1) * size] = dot(every, present, NT) / jnp.maximum(dot(every, keep, NT), 1.0)

    def prepare(g):
        for o in range(per):
            src = pl.multiple_of((me ^ offs[p * per + o]) * rb, rb)
            for q in range(g * ib, (g + 1) * ib):
                hi, lo = split(dv[q, pl.ds(src, rb), :] * f_ref[o * rb : (o + 1) * rb, q : q + 1])
                ghi[o * rb : (o + 1) * rb, q * k : (q + 1) * k] = hi
                glo[o * rb : (o + 1) * rb, q * k : (q + 1) * k] = lo

    prepare(0)
    for g in range(steps):
        if g + 1 < steps:
            prepare(g + 1)
        lanes = slice(g * ib * k, (g + 1) * ib * k)
        hi, lo = ghi[:, lanes], glo[:, lanes]
        rows = hi.shape[0]
        x = dot(jnp.concatenate([hi, lo], axis=0), thi_ref[:, lanes], NT)
        x = x[:rows] + x[rows:] + dot(hi, tlo_ref[:, lanes], NT)
        out_ref[...] = x if g == 0 else out_ref[...] + x


def b_call(me, d, thi, tlo, masks, own, offs, rb, ib, s, part):
    r, total, k = d.shape
    ws = thi.shape[0]
    rows = total // 2
    held = [pltpu.with_memory_space_constraint(x, pltpu.VMEM) for x in (d, thi, tlo)]
    return call(
        functools.partial(b_kernel, ib=ib, offs=offs, rb=rb, s=s, part=part),
        f"right_grad_{part}",
        3.7,
        6,
        in_specs=[SM] + [VM] * 5,
        out_specs=[VM] * 3,
        out_shape=[pltpu.VMEM((rows, ws), F32)] + [pltpu.VMEM((rows, r * k), BF16)] * 2,
        scratch_shapes=[pltpu.VMEM((rows, r), F32)],
    )(me, *held, masks, own)


def c_kernel(*refs, ib, s, k, steps, blocks, part, parts):
    g_refs = refs[: 2 * blocks]
    me_ref, ra_ref, rb_ref, w_ref, l_ref, lg_ref, keep_ref, send_ref, rr, xhi, xlo, acc, lt_ref, turned, wsplit = refs[2 * blocks :]
    w = l_ref.shape[1]
    wk = w * k // parts
    ws = w * s // parts
    rows = g_refs[0].shape[0]
    hi, lo = split(weights(w_ref, w, part * w // parts, w // parts))
    wsplit[:w] = hi
    wsplit[w:] = lo
    turned[...] = residues(l_ref, l_ref.shape[0] // s, s, 0, l_ref.shape[0] // s).T
    quarter = w // 4
    for t, place in enumerate(PLACES):
        at = pl.multiple_of(((me_ref[0] & 3) ^ place) * quarter, quarter)
        hi, lo = split(turned[pl.ds(at, quarter), :])
        lt_ref[t * quarter : (t + 1) * quarter] = hi.astype(F32)
        lt_ref[w + t * quarter : w + (t + 1) * quarter] = lo.astype(F32)
    for p, half in enumerate((ra_ref, rb_ref)):
        hi, lo = split(half[:, part * ws : (part + 1) * ws].T)
        rr[:ws, p * rows : (p + 1) * rows] = hi
        rr[ws:, p * rows : (p + 1) * rows] = lo

    def first(g):
        lanes = slice(g * ib * k, (g + 1) * ib * k)
        c1 = 0.0
        for p in range(blocks):
            js = slice(p * rows, (p + 1) * rows)
            x = dot(rr[:, js], g_refs[2 * p][:, lanes])
            c1 = c1 + x[:ws] + x[ws:] + dot(rr[:ws, js], g_refs[2 * p + 1][:, lanes])
        hi, lo = split(c1)
        for i in range(ib):
            q = g * ib + i
            for b in range(ws // s):
                xhi[q * s : (q + 1) * s, b * k : (b + 1) * k] = hi[b * s : (b + 1) * s, i * k : (i + 1) * k]
                xlo[q * s : (q + 1) * s, b * k : (b + 1) * k] = lo[b * s : (b + 1) * s, i * k : (i + 1) * k]

    def second(q0, q1):
        at = slice(q0 * ib * s, q1 * ib * s)
        xh, xl = xhi[at], xlo[at]
        x = dot(xh, wsplit[...], NT)
        lg_ref[at] = x[:, :w] + x[:, w:] + dot(xl, wsplit[:w], NT)
        lt = lt_ref[:, at].astype(BF16)
        x = dot(lt, xh)
        x = x[:w] + x[w:] + dot(lt[:w], xl)
        x = x if q0 == 0 else acc[...] + x
        if q1 < steps:
            acc[...] = x
        else:
            for b in range(ws // s):
                lanes = slice(b * k, (b + 1) * k)
                keep_ref[:, b, :] = x[: w // 2, lanes]
                send_ref[:, b, :] = x[w // 2 :, lanes]

    span = min(2, steps)
    for g in range(steps):
        first(g)
        if g >= span and g % span == 0:
            second(g - span, g)
    second(steps - span, steps)


def c_call(gs, me, rights, w2, left, ib, s, part, parts):
    blocks = len(gs) // 2
    total = 2 * rights[0].shape[0]
    w = left.shape[1]
    ws = w * s // parts
    k = w2.shape[1]
    r = gs[0].shape[1] // k
    wk = w * k // parts
    return call(
        functools.partial(c_kernel, ib=ib, s=s, k=k, steps=r // ib, blocks=blocks, part=part, parts=parts),
        f"left_and_weight_grad_{part}",
        5.6,
        20,
        in_specs=[VM] * (2 * blocks) + [SM, VM, VM, VM, VM],
        out_specs=[VM] * 3,
        out_shape=[pltpu.VMEM((r * s, w), F32)] + [pltpu.VMEM((w // 2, ws // s, k), F32)] * 2,
        scratch_shapes=[pltpu.VMEM((2 * ws, total), BF16)]
        + [pltpu.VMEM((r * s, wk), BF16)] * 2
        + [pltpu.VMEM((w, wk), F32), pltpu.VMEM((2 * w, r * s), F32), pltpu.VMEM((w, r * s), F32)]
        + [pltpu.VMEM((2 * w, wk), BF16)],
    )(*gs, me, *rights, w2, left)


def place_kernel(me_ref, *refs, parts):
    sources, (out_ref, sems) = refs[: 2 * parts], refs[2 * parts :]
    rows, wide = sources[0].shape[:2]
    quarter = rows // 2
    copies = []
    for part in range(parts):
        for q, place in enumerate(PLACES):
            source = sources[2 * part + q // 2].at[pl.ds((q % 2) * quarter, quarter)]
            at = pl.multiple_of(((me_ref[0] & 3) ^ place) * quarter, quarter)
            target = out_ref.at[pl.ds(at, quarter), pl.ds(part * wide, wide)]
            copies.append(pltpu.make_async_copy(source, target, sems.at[4 * part + q]))
    for copy in copies:
        copy.start()
    for copy in copies:
        copy.wait()


def place_call(me, sources):
    parts = len(sources) // 2
    rows, wide, k = sources[0].shape
    return call(
        functools.partial(place_kernel, parts=parts),
        "place_weight_grad",
        0.8,
        4,
        in_specs=[SM] + [VM] * len(sources),
        out_specs=ANY,
        out_shape=jax.ShapeDtypeStruct((2 * rows, parts * wide, k), F32),
        scratch_shapes=[pltpu.SemaphoreType.DMA((4 * parts,))],
    )(me, *sources)


def swap(x, bit, n):
    return lax.ppermute(x, "row", [(i, i ^ bit) for i in range(n)])


def gather_relative(x, bits, n):
    for bit in bits:
        x = jnp.concatenate([x, swap(x, bit, n)], axis=0)
    return x


def relative_order(bits):
    offs = [0]
    for bit in bits:
        offs = offs + [o ^ bit for o in offs]
    return tuple(offs)


def after(x, *others):
    return lax.optimization_barrier((x, *others))[0]


def local(n, activation, valid, flags, w1, w2, wf, delta):
    s, r, m = activation.shape
    total, k = delta.shape[1:]
    w = w1.shape[1]
    ib = min(8, r)
    parts = 2
    me = lax.axis_index("row").astype(jnp.int32)
    bits = [1 << e for e in reversed(range(n.bit_length() - 1))]
    offs = relative_order(bits)

    here = me.reshape(1)
    keep = valid.astype(F32)
    both = jnp.einsum("sim,mc->sic", activation, jnp.concatenate([w1, w2], axis=1), precision=EXACT)
    both = both * keep[:, :, None]
    left, right = both[:, :, :w].reshape(s * r, w), both[:, :, w:]
    ws = w * s
    own = jnp.concatenate([valid, flags[None], jnp.zeros((GAP - 1 - s, r), jnp.int32)], axis=0)
    own = with_layout_constraint(own, Layout(major_to_minor=(0, 1)))
    for bit in (1, 2):
        own = jnp.concatenate([own, swap(own, bit, n)], axis=0)
    own = own.T.astype(F32)
    masks = own
    load = jnp.concatenate([right.transpose(1, 2, 0).reshape(r, ws), own], axis=1)
    for bit in bits[:-2]:
        other = swap(load, bit, n)
        masks = jnp.concatenate([masks, other[:, ws:]], axis=0)
        load = jnp.concatenate([load[:, :ws], other[:, :ws]] if bit == bits[-3] else [load, other], axis=0)

    if r % 16 == 0:
        where, rb, blocks = here, r, offs
    else:
        order = me ^ jnp.array(offs, jnp.int32)
        delta = jnp.take(delta.reshape(r, n, r, k), order, axis=1).reshape(r, total, k)
        rb = total // 4
        where, blocks = jnp.zeros((1,), jnp.int32), tuple(range(4))

    thi, tlo, delta = t_call(delta, after(left, masks), wf, ib, s)
    far, fhi, flo = b_call(where, delta, thi, tlo, masks, own, blocks, rb, ib, s, 1)
    load = jnp.concatenate([load, after(swap(load, 2, n), far)], axis=0)
    near, nhi, nlo = b_call(after(where, load), delta, thi, tlo, masks, own, blocks, rb, ib, s, 0)
    gs = (nhi, nlo, fhi, flo)
    rights = (load, after(swap(load, 1, n), near))

    def halves(x, y, rows):
        return x[:rows] + y[:rows], x[rows:] + y[rows:]

    later = list(reversed(bits[:-1]))
    quarter = w // 4
    rows = near.shape[0] // 2
    grad, send = halves(near, after(swap(far, 1, n), near), rows)
    left_a, ow_a, send_a = c_call(gs, after(here, grad, send), rights, wf, left, ib, s, 0, parts)
    other_a = swap(send_a, 1, n)
    rows = rows // 2
    grad, send = halves(grad, after(swap(send, later[0], n), left_a), rows)
    ow_a, send_a = halves(ow_a, other_a, quarter)
    left_b, ow_b, send_b = c_call(gs, after(here, grad, send, ow_a, send_a), rights, wf, left, ib, s, 1, parts)

    ow_a = ow_a + after(swap(send_a, 2, n), left_b)
    ow_b, send_b = halves(ow_b, swap(send_b, 1, n), quarter)
    for bit in later[1:]:
        rows = rows // 2
        other = after(swap(send, bit, n), left_b)
        if bit == later[-1]:
            grad = grad + other
        else:
            grad, send = halves(grad, other, rows)
    ow_b = ow_b + swap(send_b, 2, n)

    left_grad = (left_a + left_b).reshape(r, s, w).transpose(1, 0, 2) * keep[:, :, None]
    right_grad = grad.reshape(r, w, s).transpose(2, 0, 1) * keep[:, :, None]
    grads = jnp.concatenate([left_grad, right_grad], axis=2)
    small = jnp.einsum("sim,sic->cm", activation, grads, precision=EXACT)

    def finish(x):
        for bit in reversed(bits[:-2]):
            x = x + swap(x, bit, n)
        return x

    def spread(x):
        x = jnp.concatenate([x, swap(x, 2, n)], axis=0)
        return [x, swap(x, 1, n)]

    ow_a = spread(finish(ow_a))
    ow_b = finish(ow_b)
    grads = after(grads, ow_b)
    alignment = jnp.einsum("sic,mc->sim", grads, jnp.concatenate([w1, w2], axis=1), precision=EXACT)
    for bit in reversed(bits):
        small = small + swap(small, bit, n)

    out_grad = place_call(here, ow_a + spread(ow_b)).reshape(w * w, k)
    return alignment, small[:w].T, small[w:].T, out_grad


def solution(mesh):
    in_specs = (
        P("groups", "row", None),
        P("groups", "row"),
        P(("groups", "row")),
        P(),
        P(),
        P(),
        P(("groups", "row"), None, None),
    )
    out_specs = (P("groups", "row", None), P("groups", None), P("groups", None), P("groups", None))
    body = functools.partial(local, mesh.shape["row"])
    return jax.shard_map(body, mesh=mesh, in_specs=in_specs, out_specs=out_specs, check_vma=False)
```

```python
import functools

import jax
import jax.numpy as jnp
from jax import lax
from jax.experimental import pallas as pl
from jax.experimental.pallas import tpu as pltpu
from jax.experimental.layout import Layout, with_layout_constraint
from jax.sharding import PartitionSpec as P

EXACT = lax.Precision.HIGHEST
F32, BF16 = jnp.float32, jnp.bfloat16
NT = (((1,), (1,)), ((), ()))
NN = (((1,), (0,)), ((), ()))
PLACES = (0, 2, 1, 3)
GAP = 32
VM = pl.BlockSpec(memory_space=pltpu.VMEM)
SM = pl.BlockSpec(memory_space=pltpu.SMEM)
ANY = pl.BlockSpec(memory_space=pl.ANY)


def split(x):
    hi = x.astype(BF16)
    return hi, (x - hi.astype(F32)).astype(BF16)


def split_outside(x):
    hi = lax.reduce_precision(x, 8, 7)
    return hi.astype(BF16), (x - hi).astype(BF16)


def dot(a, b, dims=NN):
    return lax.dot_general(a, b, dims, preferred_element_type=F32)


def weights(w_ref, w, first=0, size=None):
    return jnp.concatenate([w_ref[pl.ds(b, w, stride=w), :] for b in range(first, first + (size or w))], axis=1)


def residues(l_ref, r, s, first, size):
    return jnp.concatenate([l_ref[pl.ds(i, s, stride=r), :] for i in range(first, first + size)], axis=0)


def call(kernel, name, cost_us, mib, **kw):
    return pl.pallas_call(
        kernel,
        compiler_params=pltpu.CompilerParams(vmem_limit_bytes=mib << 20),
        cost_estimate=pl.CostEstimate(flops=int(cost_us * 1e9), bytes_accessed=0, transcendentals=0),
        name=name,
        **kw,
    )


def t_kernel(l_ref, w_ref, d_ref, thi_ref, tlo_ref, dv_ref, wcat, sem, *, ib, s):
    r, total, k = d_ref.shape
    w = l_ref.shape[1]
    copy = pltpu.make_async_copy(d_ref, dv_ref, sem)
    copy.start()
    hi, lo = split(weights(w_ref, w))
    wcat[:w] = hi
    wcat[w : 2 * w] = hi
    wcat[2 * w :] = lo
    for g in range(r // ib):
        left = residues(l_ref, r, s, g * ib, ib)
        hi = left.astype(BF16).astype(F32)
        hi, lo = split(dot(jnp.concatenate([hi, left - hi, hi], axis=1).astype(BF16), wcat[...]))
        for i in range(ib):
            q = g * ib + i
            for b in range(w):
                rows, lanes = slice(i * s, (i + 1) * s), slice(b * k, (b + 1) * k)
                thi_ref[b * s : (b + 1) * s, q * k : (q + 1) * k] = hi[rows, lanes]
                tlo_ref[b * s : (b + 1) * s, q * k : (q + 1) * k] = lo[rows, lanes]
    copy.wait()


def t_call(d, left, wf, ib, s):
    r, total, k = d.shape
    w = left.shape[1]
    return call(
        functools.partial(t_kernel, ib=ib, s=s),
        "left_by_weights",
        4.0,
        12,
        in_specs=[VM, VM, ANY],
        out_specs=[VM] * 3,
        out_shape=[pltpu.VMEM((w * s, r * k), BF16)] * 2 + [pltpu.VMEM(d.shape, F32)],
        scratch_shapes=[pltpu.VMEM((3 * w, w * k), BF16), pltpu.SemaphoreType.DMA],
    )(left, wf, pltpu.with_memory_space_constraint(d, pltpu.HBM))


def b_kernel(me_ref, dv, thi_ref, tlo_ref, m_ref, own_ref, out_ref, ghi, glo, f_ref, *, ib, offs, rb, s, part):
    r, total, k = dv.shape
    per = len(offs) // 2
    steps = r // ib
    me = me_ref[0]

    every = m_ref[...].astype(BF16)
    lane = lax.broadcasted_iota(jnp.int32, own_ref.shape, 1)
    p = part
    size = every.shape[0]
    for h in range(2):
        start = (2 * h + p) * GAP
        own = pltpu.roll(own_ref[...], start, 1) if start else own_ref[...]
        keep = jnp.where((lane >= start) & (lane < start + s), own, 0.0).astype(BF16)
        present = jnp.where(lane == start + s, own, 0.0).astype(BF16)
        f_ref[h * size : (h + 1) * size] = dot(every, present, NT) / jnp.maximum(dot(every, keep, NT), 1.0)

    def prepare(g):
        for o in range(per):
            src = pl.multiple_of((me ^ offs[p * per + o]) * rb, rb)
            for q in range(g * ib, (g + 1) * ib):
                hi, lo = split(dv[q, pl.ds(src, rb), :] * f_ref[o * rb : (o + 1) * rb, q : q + 1])
                ghi[o * rb : (o + 1) * rb, q * k : (q + 1) * k] = hi
                glo[o * rb : (o + 1) * rb, q * k : (q + 1) * k] = lo

    prepare(0)
    for g in range(steps):
        if g + 1 < steps:
            prepare(g + 1)
        lanes = slice(g * ib * k, (g + 1) * ib * k)
        hi, lo = ghi[:, lanes], glo[:, lanes]
        rows = hi.shape[0]
        x = dot(jnp.concatenate([hi, lo], axis=0), thi_ref[:, lanes], NT)
        x = x[:rows] + x[rows:] + dot(hi, tlo_ref[:, lanes], NT)
        out_ref[...] = x if g == 0 else out_ref[...] + x


def b_call(me, d, thi, tlo, masks, own, offs, rb, ib, s, part):
    r, total, k = d.shape
    ws = thi.shape[0]
    rows = total // 2
    held = [pltpu.with_memory_space_constraint(x, pltpu.VMEM) for x in (d, thi, tlo)]
    return call(
        functools.partial(b_kernel, ib=ib, offs=offs, rb=rb, s=s, part=part),
        f"right_grad_{part}",
        3.7,
        6,
        in_specs=[SM] + [VM] * 5,
        out_specs=[VM] * 3,
        out_shape=[pltpu.VMEM((rows, ws), F32)] + [pltpu.VMEM((rows, r * k), BF16)] * 2,
        scratch_shapes=[pltpu.VMEM((rows, r), F32)],
    )(me, *held, masks, own)


def c_kernel(*refs, ib, s, k, steps, blocks, part, parts):
    g_refs = refs[: 2 * blocks]
    me_ref, ra_ref, rb_ref, w_ref, l_ref, lg_ref, keep_ref, send_ref, rr, xhi, xlo, acc, lt_ref, turned, wsplit = refs[2 * blocks :]
    w = l_ref.shape[1]
    wk = w * k // parts
    ws = w * s // parts
    rows = g_refs[0].shape[0]
    hi, lo = split(weights(w_ref, w, part * w // parts, w // parts))
    wsplit[:w] = hi
    wsplit[w:] = lo
    turned[...] = residues(l_ref, l_ref.shape[0] // s, s, 0, l_ref.shape[0] // s).T
    quarter = w // 4
    for t, place in enumerate(PLACES):
        at = pl.multiple_of(((me_ref[0] & 3) ^ place) * quarter, quarter)
        hi, lo = split(turned[pl.ds(at, quarter), :])
        lt_ref[t * quarter : (t + 1) * quarter] = hi.astype(F32)
        lt_ref[w + t * quarter : w + (t + 1) * quarter] = lo.astype(F32)
    for p, half in enumerate((ra_ref, rb_ref)):
        hi, lo = split(half[:, part * ws : (part + 1) * ws].T)
        rr[:ws, p * rows : (p + 1) * rows] = hi
        rr[ws:, p * rows : (p + 1) * rows] = lo

    def first(g):
        lanes = slice(g * ib * k, (g + 1) * ib * k)
        c1 = 0.0
        for p in range(blocks):
            js = slice(p * rows, (p + 1) * rows)
            x = dot(rr[:, js], g_refs[2 * p][:, lanes])
            c1 = c1 + x[:ws] + x[ws:] + dot(rr[:ws, js], g_refs[2 * p + 1][:, lanes])
        hi, lo = split(c1)
        for i in range(ib):
            q = g * ib + i
            for b in range(ws // s):
                xhi[q * s : (q + 1) * s, b * k : (b + 1) * k] = hi[b * s : (b + 1) * s, i * k : (i + 1) * k]
                xlo[q * s : (q + 1) * s, b * k : (b + 1) * k] = lo[b * s : (b + 1) * s, i * k : (i + 1) * k]

    def second(q0, q1):
        at = slice(q0 * ib * s, q1 * ib * s)
        xh, xl = xhi[at], xlo[at]
        x = dot(xh, wsplit[...], NT)
        lg_ref[at] = x[:, :w] + x[:, w:] + dot(xl, wsplit[:w], NT)
        lt = lt_ref[:, at].astype(BF16)
        x = dot(lt, xh)
        x = x[:w] + x[w:] + dot(lt[:w], xl)
        x = x if q0 == 0 else acc[...] + x
        if q1 < steps:
            acc[...] = x
        else:
            for b in range(ws // s):
                lanes = slice(b * k, (b + 1) * k)
                keep_ref[:, b, :] = x[: w // 2, lanes]
                send_ref[:, b, :] = x[w // 2 :, lanes]

    span = min(2, steps)
    for g in range(steps):
        first(g)
        if g >= span and g % span == 0:
            second(g - span, g)
    second(steps - span, steps)


def c_call(gs, me, rights, w2, left, ib, s, part, parts):
    blocks = len(gs) // 2
    total = 2 * rights[0].shape[0]
    w = left.shape[1]
    ws = w * s // parts
    k = w2.shape[1]
    r = gs[0].shape[1] // k
    wk = w * k // parts
    return call(
        functools.partial(c_kernel, ib=ib, s=s, k=k, steps=r // ib, blocks=blocks, part=part, parts=parts),
        f"left_and_weight_grad_{part}",
        5.6,
        20,
        in_specs=[VM] * (2 * blocks) + [SM, VM, VM, VM, VM],
        out_specs=[VM] * 3,
        out_shape=[pltpu.VMEM((r * s, w), F32)] + [pltpu.VMEM((w // 2, ws // s, k), F32)] * 2,
        scratch_shapes=[pltpu.VMEM((2 * ws, total), BF16)]
        + [pltpu.VMEM((r * s, wk), BF16)] * 2
        + [pltpu.VMEM((w, wk), F32), pltpu.VMEM((2 * w, r * s), F32), pltpu.VMEM((w, r * s), F32)]
        + [pltpu.VMEM((2 * w, wk), BF16)],
    )(*gs, me, *rights, w2, left)


def place_kernel(me_ref, *refs, parts):
    sources, (out_ref, sems) = refs[: 2 * parts], refs[2 * parts :]
    rows, wide = sources[0].shape[:2]
    quarter = rows // 2
    copies = []
    for part in range(parts):
        for q, place in enumerate(PLACES):
            source = sources[2 * part + q // 2].at[pl.ds((q % 2) * quarter, quarter)]
            at = pl.multiple_of(((me_ref[0] & 3) ^ place) * quarter, quarter)
            target = out_ref.at[pl.ds(at, quarter), pl.ds(part * wide, wide)]
            copies.append(pltpu.make_async_copy(source, target, sems.at[4 * part + q]))
    for copy in copies:
        copy.start()
    for copy in copies:
        copy.wait()


def place_call(me, sources):
    parts = len(sources) // 2
    rows, wide, k = sources[0].shape
    return call(
        functools.partial(place_kernel, parts=parts),
        "place_weight_grad",
        0.8,
        4,
        in_specs=[SM] + [VM] * len(sources),
        out_specs=ANY,
        out_shape=jax.ShapeDtypeStruct((2 * rows, parts * wide, k), F32),
        scratch_shapes=[pltpu.SemaphoreType.DMA((4 * parts,))],
    )(me, *sources)


def swap(x, bit, n):
    return lax.ppermute(x, "row", [(i, i ^ bit) for i in range(n)])


def gather_relative(x, bits, n):
    for bit in bits:
        x = jnp.concatenate([x, swap(x, bit, n)], axis=0)
    return x


def relative_order(bits):
    offs = [0]
    for bit in bits:
        offs = offs + [o ^ bit for o in offs]
    return tuple(offs)


def after(x, *others):
    return lax.optimization_barrier((x, *others))[0]


def local(n, activation, valid, flags, w1, w2, wf, delta):
    s, r, m = activation.shape
    total, k = delta.shape[1:]
    w = w1.shape[1]
    ib = min(8, r)
    parts = 2
    me = lax.axis_index("row").astype(jnp.int32)
    bits = [1 << e for e in reversed(range(n.bit_length() - 1))]
    offs = relative_order(bits)

    here = me.reshape(1)
    keep = valid.astype(F32)
    both = jnp.einsum("sim,mc->sic", activation, jnp.concatenate([w1, w2], axis=1), precision=EXACT)
    both = both * keep[:, :, None]
    left, right = both[:, :, :w].reshape(s * r, w), both[:, :, w:]
    ws = w * s
    own = jnp.concatenate([valid, flags[None], jnp.zeros((GAP - 1 - s, r), jnp.int32)], axis=0)
    own = with_layout_constraint(own, Layout(major_to_minor=(0, 1)))
    for bit in (1, 2):
        own = jnp.concatenate([own, swap(own, bit, n)], axis=0)
    own = own.T.astype(F32)
    masks = own
    load = jnp.concatenate([right.transpose(1, 2, 0).reshape(r, ws), own], axis=1)
    for bit in bits[:-2]:
        other = swap(load, bit, n)
        masks = jnp.concatenate([masks, other[:, ws:]], axis=0)
        load = jnp.concatenate([load[:, :ws], other[:, :ws]] if bit == bits[-3] else [load, other], axis=0)

    if r % 16 == 0:
        where, rb, blocks = here, r, offs
    else:
        order = me ^ jnp.array(offs, jnp.int32)
        delta = jnp.take(delta.reshape(r, n, r, k), order, axis=1).reshape(r, total, k)
        rb = total // 4
        where, blocks = jnp.zeros((1,), jnp.int32), tuple(range(4))

    thi, tlo, delta = t_call(delta, after(left, masks), wf, ib, s)
    far, fhi, flo = b_call(where, delta, thi, tlo, masks, own, blocks, rb, ib, s, 1)
    load = jnp.concatenate([load, after(swap(load, 2, n), far)], axis=0)
    near, nhi, nlo = b_call(after(where, load), delta, thi, tlo, masks, own, blocks, rb, ib, s, 0)
    gs = (nhi, nlo, fhi, flo)
    rights = (load, after(swap(load, 1, n), near))

    def halves(x, y, rows):
        return x[:rows] + y[:rows], x[rows:] + y[rows:]

    later = list(reversed(bits[:-1]))
    quarter = w // 4
    rows = near.shape[0] // 2
    grad, send = halves(near, after(swap(far, 1, n), near), rows)
    left_a, ow_a, send_a = c_call(gs, after(here, grad, send), rights, wf, left, ib, s, 0, parts)
    other_a = swap(send_a, 1, n)
    rows = rows // 2
    grad, send = halves(grad, after(swap(send, later[0], n), left_a), rows)
    ow_a, send_a = halves(ow_a, other_a, quarter)
    left_b, ow_b, send_b = c_call(gs, after(here, grad, send, ow_a, send_a), rights, wf, left, ib, s, 1, parts)

    ow_a = ow_a + after(swap(send_a, 2, n), left_b)
    ow_b, send_b = halves(ow_b, swap(send_b, 1, n), quarter)
    for bit in later[1:]:
        rows = rows // 2
        other = after(swap(send, bit, n), left_b, send_b) if bit == later[-1] else after(swap(send, bit, n), left_b)
        if bit == later[-1]:
            grad = grad + other
        else:
            grad, send = halves(grad, other, rows)
    ow_b = ow_b + swap(send_b, 2, n)

    left_grad = (left_a + left_b).reshape(r, s, w).transpose(1, 0, 2) * keep[:, :, None]
    right_grad = grad.reshape(r, w, s).transpose(2, 0, 1) * keep[:, :, None]
    grads = jnp.concatenate([left_grad, right_grad], axis=2)
    small = jnp.einsum("sim,sic->cm", activation, grads, precision=EXACT)

    def finish(x):
        for bit in reversed(bits[:-2]):
            x = x + swap(x, bit, n)
        return x

    def spread(x):
        x = jnp.concatenate([x, swap(x, 2, n)], axis=0)
        return [x, swap(x, 1, n)]

    ow_a = spread(finish(ow_a))
    ow_b = finish(ow_b)
    grads = after(grads, ow_b)
    alignment = jnp.einsum("sic,mc->sim", grads, jnp.concatenate([w1, w2], axis=1), precision=EXACT)
    for bit in (*reversed(bits[:-1]), 1):
        small = small + swap(small, bit, n)

    out_grad = place_call(here, ow_a + spread(ow_b)).reshape(w * w, k)
    return alignment, small[:w].T, small[w:].T, out_grad


def solution(mesh):
    in_specs = (
        P("groups", "row", None),
        P("groups", "row"),
        P(("groups", "row")),
        P(),
        P(),
        P(),
        P(("groups", "row"), None, None),
    )
    out_specs = (P("groups", "row", None), P("groups", None), P("groups", None), P("groups", None))
    body = functools.partial(local, mesh.shape["row"])
    return jax.shard_map(body, mesh=mesh, in_specs=in_specs, out_specs=out_specs, check_vma=False)
```
